256 devices in a mesh: shard: 64 (over y, z, core), sub: 4 (over x).
Axes of the slice: x: 4, y: 4, z: 8, core: 2. Of those that a mesh axis runs over, the one named last changes fastest.
Arguments:
- points: bfloat16 [262144, 768], P(('shard', 'sub'))
- centroids: float32 [262144, 768], P(('shard', 'sub')), may hold values from -6 to 6
- cand_peer: int32 [1024, 4], P(('shard', 'sub')), may hold values from 0 to 63, as said below
- cand_block: int32 [1024, 4], P(('shard', 'sub')), may hold values from 0 to 7
Outputs:
- refined: float32 [262144, 768], P(('shard', 'sub'))
The draws below stay inside these ranges and needn't reach their ends.
Inputs may be any that keep to these rules, and one draw needn't show every extreme that they name: The owner of a candidate is the device with shard index cand_peer and the sub index of the requesting device. The 4 peers of one point block differ. All requests of one device to one peer name the same block.
All inputs are finite; a program needn't handle non-finite values.
Results may differ from the reference program's by a relative error of at most 0.0011.
Values may be sent and summed in bfloat16 or wider, within the bound.
A program may use at most 128 MiB of HBM per device.

```python
import jax
import jax.numpy as jnp
from jax import lax

D = 768
PBLK = 256
CBLK = 128
CAND = 4
P_DEV = 1024
CB_DEV = 8
POINTS = 262144
CENTS = 262144
N_SHARD = 64
N_SUB = 4


def shared_requests(key):
    nblk = POINTS // PBLK
    per = P_DEV // PBLK
    ndev = POINTS // P_DEV
    first, second = jax.random.split(key)
    scores = jax.random.randint(first, (nblk, N_SHARD), 0, 2 ** 20) * N_SHARD + jnp.arange(N_SHARD, dtype=jnp.int32)[None, :]
    picked = lax.top_k(scores, CAND)[1].astype(jnp.int32)
    table = jax.random.randint(second, (ndev, N_SHARD), 0, CB_DEV).astype(jnp.int32)
    device = jnp.arange(nblk, dtype=jnp.int32) // per
    blocks = table[device[:, None], picked]
    return (picked, blocks)


def draw_cand_peer(key, part):
    picked, blocks = shared_requests(key)
    return picked


def draw_cand_block(key, part):
    picked, blocks = shared_requests(key)
    return blocks


def draw_points(key, part):
    key = jax.random.fold_in(key, 7)
    first, second = jax.random.split(key, 2)
    ndev = POINTS // P_DEV
    device = (jnp.arange(POINTS) // P_DEV).astype(jnp.float32)
    lift = 1.0 + 2.0 * device / max(ndev - 1, 1)
    rough = jax.random.uniform(second, (POINTS, 1), jnp.float32, 0.6, 1.4)
    values = jnp.clip(jax.random.normal(first, (POINTS, D), jnp.float32), -6.0, 6.0)
    return (values * rough * lift[:, None]).astype(jnp.bfloat16)


def level_of(own_key, dims, cuts, low, largest):
    def one(axis_at, parts):
        heights = jax.random.uniform(jax.random.fold_in(jax.random.fold_in(own_key, 6), axis_at), (parts,), jnp.float32, low / len(cuts), largest / len(cuts))
        return jnp.repeat(jnp.exp(heights), dims[axis_at] // parts).reshape((-1,) + (1,) * (len(dims) - axis_at - 1))

    gain = one(*cuts[0])
    for cut in cuts[1:]:
        gain = gain * one(*cut)
    return gain


def normal_values(own_key, extent, scale, limit, cuts=(), held_as=jnp.bfloat16):
    gain = level_of(own_key, extent, cuts, -0.22, 0.18) if cuts else 1.0
    drawn = jax.random.normal(own_key, extent, jnp.float32) * scale * gain
    return jnp.minimum(jnp.maximum(drawn, -limit), limit).astype(held_as)


def setup_inputs(seed: int = 0) -> dict:
    seeds = jax.random.split(jax.random.key(seed), 5)
    points = draw_points(jax.random.fold_in(seeds[4], 71), 0)
    centroids = normal_values(seeds[1], (CENTS, D), 1.0, 6.0, ((0, 256),), jnp.float32)
    cand_peer = draw_cand_peer(jax.random.fold_in(seeds[4], 71), 0)
    cand_block = draw_cand_block(jax.random.fold_in(seeds[4], 71), 0)
    return {"points": points, "centroids": centroids, "cand_peer": cand_peer, "cand_block": cand_block}


def reference(points, centroids, cand_peer, cand_block):
    per = P_DEV // PBLK
    nblk = points.shape[0] // PBLK
    ndev = points.shape[0] // P_DEV
    nown = centroids.shape[0] // CBLK
    width = points.shape[1]
    half = centroids.astype(jnp.bfloat16)
    csq = jnp.sum(half.astype(jnp.float32) ** 2, axis=-1)
    xsq = jnp.sum(points.astype(jnp.float32) ** 2, axis=-1)
    device = jnp.arange(nblk, dtype=jnp.int32) // per
    owner = cand_peer * N_SUB + (device % N_SUB)[:, None]
    start = (owner * CB_DEV + cand_block) * CBLK
    offsets = jnp.arange(CBLK, dtype=jnp.int32)
    peers = jnp.arange(N_SHARD, dtype=jnp.int32)

    def distances(index):
        rows = lax.dynamic_slice_in_dim(points, (index * PBLK).astype(jnp.int32), PBLK, 0)
        sqrs = lax.dynamic_slice_in_dim(xsq, (index * PBLK).astype(jnp.int32), PBLK, 0)
        columns = (start[index][:, None] + offsets[None, :]).reshape(-1)
        chosen = half[columns]
        dots = jnp.dot(rows, chosen.T, preferred_element_type=jnp.float32)
        dist = sqrs[:, None] + csq[columns][None, :] - 2.0 * dots
        return dist, rows

    def gap_of(index):
        dist, rows = distances(index)
        return jnp.sum(jnp.mean(dist, axis=1) - jnp.min(dist, axis=1))

    gaps = lax.map(gap_of, jnp.arange(nblk, dtype=jnp.int32))
    spread = jnp.sum(gaps) / points.shape[0] + 1e-6

    def device_step(carry, dev):
        sums, weights = carry

        def block_step(local, inner):
            index = (dev * per + inner).astype(jnp.int32)
            dist, rows = distances(index)
            logits = -3.0 * (dist - jnp.min(dist, axis=1, keepdims=True)) / spread
            resp = jax.nn.softmax(logits, axis=1).astype(jnp.bfloat16)
            part = jnp.dot(resp.T, rows, preferred_element_type=jnp.float32).reshape(CAND, CBLK, width)
            mass = jnp.sum(resp.astype(jnp.float32), axis=0).reshape(CAND, CBLK)
            lsum, lmass = local
            return (lsum.at[cand_peer[index]].add(part), lmass.at[cand_peer[index]].add(mass)), None

        init = (jnp.zeros((N_SHARD, CBLK, width), jnp.float32), jnp.zeros((N_SHARD, CBLK), jnp.float32))
        (lsum, lmass), _ = lax.scan(block_step, init, jnp.arange(per, dtype=jnp.int32))
        lsum = lax.optimization_barrier(lsum.astype(jnp.bfloat16)).astype(jnp.float32)
        lmass = lax.optimization_barrier(lmass.astype(jnp.bfloat16)).astype(jnp.float32)
        mine = lax.dynamic_slice_in_dim(cand_peer, (dev * per).astype(jnp.int32), per, 0)
        which = lax.dynamic_slice_in_dim(cand_block, (dev * per).astype(jnp.int32), per, 0)
        hits = mine[:, :, None] == peers[None, None, :]
        wanted = jnp.max(jnp.where(hits, which[:, :, None], -1), axis=(0, 1)).astype(jnp.int32)
        target = ((peers * N_SUB + dev % N_SUB) * CB_DEV + jnp.maximum(wanted, 0)).astype(jnp.int32)
        return (sums.at[target].add(lsum), weights.at[target].add(lmass)), None

    init = (jnp.zeros((nown, CBLK, width), jnp.float32), jnp.zeros((nown, CBLK), jnp.float32))
    (sums, weights), _ = lax.scan(device_step, init, jnp.arange(ndev, dtype=jnp.int32))
    sums = sums.reshape(centroids.shape)
    weights = weights.reshape(-1)
    return (sums + 1.0 * centroids) / (weights + 1.0)[:, None]
```

```python
import functools

import jax
import jax.numpy as jnp
from jax import lax
from jax.experimental import pallas as pl
from jax.experimental.pallas import tpu as pltpu
from jax.sharding import PartitionSpec as P

PBLK = 256
CBLK = 128
CAND = 4
NY, NZ, NC = 4, 8, 2
NQ = 3
LANES = 128
OWNED = 8
SLOTS = 16
VMEM_LIMIT = 60 * 1024 * 1024
MESH = pl.DeviceIdType.MESH


def wait_bytes(ref, sem):
    pltpu.make_async_copy(ref, ref, sem).wait()


def kernel(
    ny,
    nz,
    nx,
    total_points,
    x_ref,
    h_ref,
    xsq_ref,
    req_ref,
    mask_ref,
    out_ref,
    outw_ref,
    rq,
    onehot,
    onehot_t,
    held,
    pick,
    got,
    dist,
    csq,
    resp,
    back,
    part,
    final,
    home,
    w_pick,
    w_back,
    w_sum,
    w_part,
    w_final,
    w_home,
    gap_own,
    gap_row,
    gap_y,
    gap_x,
    send_sem,
    recv_sem,
):
    nk = nz * NC
    rp = CBLK // nz // 2
    pts = x_ref.shape[0]
    keys = ny * nk * SLOTS
    f32 = jnp.float32
    bf16 = jnp.bfloat16
    shard = lax.axis_index("shard")
    sub = lax.axis_index("sub")
    my_y = lax.div(shard, nk)
    my_k = lax.rem(shard, nk)

    def row_dev(k):
        return (my_y * nk + k, sub)

    def y_dev(y):
        return (y * nk + my_k, sub)

    barrier = pltpu.get_barrier_semaphore()

    def greet_row(off, carry):
        pl.semaphore_signal(
            barrier, inc=1, device_id=row_dev(lax.rem(my_k + off, nk)), device_id_type=MESH
        )
        return carry

    lax.fori_loop(1, nk, greet_row, 0)
    for off in range(1, ny):
        pl.semaphore_signal(
            barrier, inc=1, device_id=y_dev(lax.rem(my_y + off, ny)), device_id_type=MESH
        )
    for off in range(1, nx):
        pl.semaphore_signal(
            barrier, inc=1, device_id=(shard, lax.rem(sub + off, nx)), device_id_type=MESH
        )
    pl.semaphore_wait(barrier, nk - 1 + ny - 1 + nx - 1)

    def row_send(src_of, dst_of, sem):
        def body(off, carry):
            k = lax.rem(my_k + off, nk)
            pltpu.make_async_remote_copy(
                src_ref=src_of(k),
                dst_ref=dst_of(my_k),
                send_sem=send_sem.at[sem],
                recv_sem=recv_sem.at[sem],
                device_id=row_dev(k),
                device_id_type=MESH,
            ).start()
            return carry

        lax.fori_loop(1, nk, body, 0)
        pltpu.make_async_copy(src_of(my_k), dst_of(my_k), recv_sem.at[sem]).start()

    def y_send(src_of, dst_ref, sem):
        for off in range(1, ny):
            y = lax.rem(my_y + off, ny)
            pltpu.make_async_remote_copy(
                src_ref=src_of(y),
                dst_ref=dst_ref,
                send_sem=send_sem.at[sem],
                recv_sem=recv_sem.at[sem],
                device_id=y_dev(y),
                device_id_type=MESH,
            ).start()

    REQ, GAP_ROW, GAP_Y, GAP_X, W4, W5, W6 = 0, 1, 2, 3, 4, 5, 6
    S1, S2, S3, S4, S5, S6 = (7 + NQ * s for s in range(6))

    row_send(lambda k: req_ref, lambda k: rq.at[k], REQ)
    for q in range(NQ):
        row_send(lambda k: h_ref.at[q, k], lambda k: held.at[q, my_y, k], S1 + q)

    wait_bytes(rq, recv_sem.at[REQ])

    def build(d, carry):
        code = rq[d]
        lane = lax.broadcasted_iota(jnp.int32, (SLOTS, LANES), 1)
        for t in range(keys // LANES):
            for par in range(2):
                hit = code + OWNED * par == lane + t * LANES
                onehot[d, par * SLOTS : (par + 1) * SLOTS, t * LANES : (t + 1) * LANES] = (
                    jnp.where(hit, 1.0, 0.0).astype(bf16)
                )
        return carry

    lax.fori_loop(0, nk, build, 0)
    for t in range(nk * 2 * SLOTS // LANES):
        block = onehot[4 * t : 4 * t + 4].reshape(LANES, keys).astype(f32)
        onehot_t[:, t * LANES : (t + 1) * LANES] = block.T.astype(bf16)

    for q in range(NQ):
        wait_bytes(held.at[q, my_y], recv_sem.at[S1 + q])
        y_send(lambda y: held.at[q, my_y], held.at[q, my_y], S2 + q)

    for q in range(NQ):
        wait_bytes(held.at[q, pl.ds(0, ny - 1)], recv_sem.at[S2 + q])

        def select(p, carry):
            left = held[q, :, :, 2 * p].reshape(keys, LANES)
            right = held[q, :, :, 2 * p + 1].reshape(keys, LANES)
            both = jnp.concatenate([left, right], axis=1)
            table = onehot[...].reshape(nk * 2 * SLOTS, keys)
            chosen = jnp.dot(table, both, preferred_element_type=f32).astype(bf16)
            pick[q, :, 2 * p] = chosen[:, :LANES].reshape(nk, 2 * SLOTS, LANES)
            pick[q, :, 2 * p + 1] = chosen[:, LANES:].reshape(nk, 2 * SLOTS, LANES)
            return carry

        lax.fori_loop(0, rp // 2, select, 0)
        row_send(lambda k: pick.at[q, k], lambda k: got.at[q, k], S3 + q)

    rows = rp * 2 * SLOTS
    for q in range(NQ):
        wait_bytes(got.at[q], recv_sem.at[S3 + q])

        def multiply(g, carry):
            left = got[q, 2 * g].reshape(rows, LANES)
            right = got[q, 2 * g + 1].reshape(rows, LANES)
            both = jnp.concatenate([left, right], axis=1)
            dots = lax.dot_general(
                both,
                x_ref[:, q * 2 * LANES : (q + 1) * 2 * LANES],
                (((1,), (1,)), ((), ())),
                preferred_element_type=f32,
            ).reshape(2 * rp, SLOTS, pts)
            square = jnp.square(left.astype(f32)) + jnp.square(right.astype(f32))
            square = square.reshape(2 * rp, SLOTS, LANES)
            here = pl.ds(g * 2 * rp, 2 * rp)
            if q == 0:
                dist[here] = dots
                csq[here] = square
            else:
                dist[here] = dist[here] + dots
                csq[here] = csq[here] + square
            return carry

        lax.fori_loop(0, nz, multiply, 0)

    groups = nz * 2 * rp

    def measure(i, carry):
        least, total = carry
        valid = mask_ref[...] > 0.5
        col = jnp.sum(csq[i], axis=1, keepdims=True)
        d = (xsq_ref[...] + col) - 2.0 * dist[i]
        far = jnp.where(valid, d, jnp.inf)
        dist[i] = far
        return jnp.minimum(least, far), total + jnp.where(valid, d, 0.0)

    least, total = lax.fori_loop(
        0,
        groups,
        measure,
        (jnp.full((SLOTS, pts), jnp.inf, f32), jnp.zeros((SLOTS, pts), f32)),
    )
    least = jnp.min(least, axis=0, keepdims=True)
    total = jnp.sum(total, axis=0, keepdims=True)
    gap = jnp.sum(total / (CAND * CBLK) - least, axis=1, keepdims=True)

    gap_own[0] = jnp.broadcast_to(gap, (8, LANES))
    row_send(lambda k: gap_own.at[0], lambda k: gap_row.at[k], GAP_ROW)
    wait_bytes(gap_row, recv_sem.at[GAP_ROW])
    gap_own[1] = jnp.sum(gap_row[...], axis=0)
    gap_y[my_y] = gap_own[1]
    y_send(lambda y: gap_own.at[1], gap_y.at[my_y], GAP_Y)
    wait_bytes(gap_y.at[pl.ds(0, ny - 1)], recv_sem.at[GAP_Y])
    gap_own[2] = jnp.sum(gap_y[...], axis=0)
    gap_x[sub] = gap_own[2]
    for off in range(1, nx):
        pltpu.make_async_remote_copy(
            src_ref=gap_own.at[2],
            dst_ref=gap_x.at[sub],
            send_sem=send_sem.at[GAP_X],
            recv_sem=recv_sem.at[GAP_X],
            device_id=(shard, lax.rem(sub + off, nx)),
            device_id_type=MESH,
        ).start()
    if nx > 1:
        wait_bytes(gap_x.at[pl.ds(0, nx - 1)], recv_sem.at[GAP_X])
    spread = jnp.sum(gap_x[...], axis=0)[:1, :1] / total_points + 1e-6
    scale = 3.0 / spread

    def exponent(i, norm):
        e = jnp.exp((least - dist[i]) * scale)
        dist[i] = e
        return norm + e

    norm = lax.fori_loop(0, groups, exponent, jnp.zeros((SLOTS, pts), f32))
    inverse = 1.0 / jnp.sum(norm, axis=0, keepdims=True)

    def normalise(i, carry):
        resp[i] = (dist[i] * inverse).astype(bf16)
        return carry

    lax.fori_loop(0, groups, normalise, 0)

    for q in range(NQ):
        wait_bytes(pick.at[q, pl.ds(0, nk - 1)], send_sem.at[S3 + q])

        def accumulate(g, carry):
            here = resp[pl.ds(g * 2 * rp, 2 * rp)].reshape(rows, pts)
            sums = jnp.dot(
                here, x_ref[:, q * 2 * LANES : (q + 1) * 2 * LANES], preferred_element_type=f32
            ).astype(bf16)
            pick[q, 2 * g] = sums[:, :LANES].reshape(rp, 2 * SLOTS, LANES)
            pick[q, 2 * g + 1] = sums[:, LANES:].reshape(rp, 2 * SLOTS, LANES)
            if q == 0:
                mass = jnp.dot(here, jnp.ones((pts, LANES), bf16), preferred_element_type=f32)
                mass = mass.reshape(rp, 2 * SLOTS, LANES)
                lane = lax.broadcasted_iota(jnp.int32, (2 * SLOTS, LANES), 1)
                packed = jnp.zeros((2 * SLOTS, LANES), f32)
                for r in range(rp):
                    packed = jnp.where(lane == r, mass[r], packed)
                w_pick[g] = packed.astype(bf16)
            return carry

        lax.fori_loop(0, nz, accumulate, 0)
        row_send(lambda k: pick.at[q, k], lambda k: back.at[q, k], S4 + q)
    row_send(lambda k: w_pick.at[lax.div(k, NC)], lambda k: w_back.at[k], W4)

    for q in range(NQ):
        wait_bytes(held.at[q, pl.ds(0, ny - 1)], send_sem.at[S2 + q])
        wait_bytes(back.at[q], recv_sem.at[S4 + q])

        def combine(p, carry):
            left = back[q, :, 2 * p].reshape(nk * 2 * SLOTS, LANES)
            right = back[q, :, 2 * p + 1].reshape(nk * 2 * SLOTS, LANES)
            both = jnp.concatenate([left, right], axis=1)
            added = jnp.dot(onehot_t[...], both, preferred_element_type=f32).astype(bf16)
            held[q, :, :, 2 * p] = added[:, :LANES].reshape(ny, nk, SLOTS, LANES)
            held[q, :, :, 2 * p + 1] = added[:, LANES:].reshape(ny, nk, SLOTS, LANES)
            return carry

        lax.fori_loop(0, rp // 2, combine, 0)
        y_send(lambda y: held.at[q, y], part.at[q, my_y], S5 + q)
    wait_bytes(w_back, recv_sem.at[W4])
    w_sum[...] = jnp.dot(
        onehot_t[...], w_back[...].reshape(nk * 2 * SLOTS, LANES), preferred_element_type=f32
    ).reshape(ny, nk, SLOTS, LANES)
    y_send(lambda y: w_sum.at[y], w_part.at[my_y], W5)

    for q in range(NQ):
        wait_bytes(part.at[q, pl.ds(0, ny - 1)], recv_sem.at[S5 + q])

        def gather(k, carry):
            added = held[q, my_y, k].astype(f32)
            for off in range(1, ny):
                added = added + part[q, lax.rem(my_y + off, ny), k].astype(f32)
            final[q, k] = added.astype(bf16)
            return carry

        lax.fori_loop(0, nk, gather, 0)
        row_send(lambda k: final.at[q, k], lambda k: home.at[q, k], S6 + q)
    wait_bytes(w_part.at[pl.ds(0, ny - 1)], recv_sem.at[W5])
    weight = w_sum[my_y]
    for off in range(1, ny):
        weight = weight + w_part[lax.rem(my_y + off, ny)]
    w_final[...] = weight
    row_send(lambda k: w_final.at[k], lambda k: w_home.at[k], W6)

    for q in range(NQ):
        wait_bytes(home.at[q], recv_sem.at[S6 + q])
        out_ref[q] = home[q]
    wait_bytes(w_home, recv_sem.at[W6])
    outw_ref[...] = w_home[...]

    wait_bytes(rq.at[pl.ds(0, nk - 1)], send_sem.at[REQ])
    wait_bytes(gap_row.at[pl.ds(0, nk - 1)], send_sem.at[GAP_ROW])
    wait_bytes(gap_y.at[pl.ds(0, ny - 1)], send_sem.at[GAP_Y])
    if nx > 1:
        wait_bytes(gap_x.at[pl.ds(0, nx - 1)], send_sem.at[GAP_X])
    wait_bytes(w_back.at[pl.ds(0, nk - 1)], send_sem.at[W4])
    wait_bytes(w_sum.at[pl.ds(0, ny - 1)], send_sem.at[W5])
    wait_bytes(w_final.at[pl.ds(0, nk - 1)], send_sem.at[W6])
    for q in range(NQ):
        wait_bytes(h_ref.at[q, pl.ds(0, nk - 1)], send_sem.at[S1 + q])
        wait_bytes(pick.at[q, pl.ds(0, nk - 1)], send_sem.at[S4 + q])
        wait_bytes(held.at[q, pl.ds(0, ny - 1)], send_sem.at[S5 + q])
        wait_bytes(final.at[q, pl.ds(0, nk - 1)], send_sem.at[S6 + q])


def on_device(ny, nz, nx, points, centroids, cand_peer, cand_block):
    f32, bf16 = jnp.float32, jnp.bfloat16
    nk = nz * NC
    rp = CBLK // nz // 2
    pts, width = points.shape
    blocks_here = pts // PBLK
    total_points = pts * ny * nk * nx
    keys = ny * nk * SLOTS

    peer = cand_peer.reshape(-1)
    same = peer[:, None] == peer[None, :]
    before = jnp.arange(SLOTS)[None, :] < jnp.arange(SLOTS)[:, None]
    first = jnp.logical_not(jnp.any(same & before, axis=1))
    code = jnp.where(first, peer * SLOTS + cand_block.reshape(-1), -(2**20)).astype(jnp.int32)
    req = jnp.broadcast_to(code[:, None], (SLOTS, LANES))
    used = jnp.any(same.reshape(SLOTS, blocks_here, CAND), axis=2) & first[:, None]
    mask = jnp.repeat(used.astype(f32), PBLK, axis=1)

    half = centroids.astype(bf16).reshape(OWNED, nz, rp, 2, NQ, NC, LANES)
    half = half.transpose(4, 1, 5, 2, 3, 0, 6).reshape(NQ, nk, rp, SLOTS, LANES)
    xsq = jnp.sum(jnp.square(points.astype(f32)), axis=1)[None, :]

    vmem = pl.BlockSpec(memory_space=pltpu.VMEM)
    n_sem = 7 + 6 * NQ
    sums, weights = pl.pallas_call(
        functools.partial(kernel, ny, nz, nx, total_points),
        out_shape=(
            jax.ShapeDtypeStruct((NQ, nk, rp, SLOTS, LANES), bf16),
            jax.ShapeDtypeStruct((nk, SLOTS, LANES), f32),
        ),
        in_specs=[vmem] * 5,
        out_specs=(vmem, vmem),
        scratch_shapes=[
            pltpu.VMEM((nk, SLOTS, LANES), jnp.int32),
            pltpu.VMEM((nk, 2 * SLOTS, keys), bf16),
            pltpu.VMEM((keys, nk * 2 * SLOTS), bf16),
            pltpu.VMEM((NQ, ny, nk, rp, SLOTS, LANES), bf16),
            pltpu.VMEM((NQ, nk, rp, 2 * SLOTS, LANES), bf16),
            pltpu.VMEM((NQ, nk, rp, 2 * SLOTS, LANES), bf16),
            pltpu.VMEM((nz * 2 * rp, SLOTS, pts), f32),
            pltpu.VMEM((nz * 2 * rp, SLOTS, LANES), f32),
            pltpu.VMEM((nz * 2 * rp, SLOTS, pts), bf16),
            pltpu.VMEM((NQ, nk, rp, 2 * SLOTS, LANES), bf16),
            pltpu.VMEM((NQ, ny, nk, rp, SLOTS, LANES), bf16),
            pltpu.VMEM((NQ, nk, rp, SLOTS, LANES), bf16),
            pltpu.VMEM((NQ, nk, rp, SLOTS, LANES), bf16),
            pltpu.VMEM((nz, 2 * SLOTS, LANES), bf16),
            pltpu.VMEM((nk, 2 * SLOTS, LANES), bf16),
            pltpu.VMEM((ny, nk, SLOTS, LANES), f32),
            pltpu.VMEM((ny, nk, SLOTS, LANES), f32),
            pltpu.VMEM((nk, SLOTS, LANES), f32),
            pltpu.VMEM((nk, SLOTS, LANES), f32),
            pltpu.VMEM((3, 8, LANES), f32),
            pltpu.VMEM((nk, 8, LANES), f32),
            pltpu.VMEM((ny, 8, LANES), f32),
            pltpu.VMEM((nx, 8, LANES), f32),
            pltpu.SemaphoreType.DMA((n_sem,)),
            pltpu.SemaphoreType.DMA((n_sem,)),
        ],
        compiler_params=pltpu.CompilerParams(
            collective_id=0, has_side_effects=True, vmem_limit_bytes=VMEM_LIMIT
        ),
    )(points, half, xsq, req, mask)

    sums = sums.reshape(NQ, nz, NC, rp, 2, OWNED, LANES).transpose(5, 1, 3, 4, 0, 2, 6)
    sums = sums.reshape(OWNED * CBLK, width).astype(f32)
    weights = weights.reshape(nz, NC, 2, OWNED, LANES)[:, 0, :, :, :rp].transpose(2, 0, 3, 1)
    weights = weights.reshape(OWNED * CBLK)
    return (sums + 1.0 * centroids) / (weights + 1.0)[:, None]


def solution(mesh):
    placed = P(("shard", "sub"), None)
    body = functools.partial(on_device, NY, NZ, mesh.shape["sub"])
    return jax.shard_map(
        body, mesh=mesh, in_specs=(placed,) * 4, out_specs=placed, check_vma=False
    )
```

```python
import functools

import jax
import jax.numpy as jnp
from jax import lax
from jax.experimental import pallas as pl
from jax.experimental.pallas import tpu as pltpu
from jax.sharding import PartitionSpec as P

PBLK = 256
CBLK = 128
CAND = 4
NBLK = 4
OWNED = 8
PAIRS = CBLK // 2
ROWS = 2 * OWNED
SLOTS = 2 * NBLK * CAND
NQ = 3
WIDE = 256
LANES = 128
VMEM_LIMIT = 56 * 1024 * 1024
MESH = pl.DeviceIdType.MESH
F32 = jnp.float32
BF16 = jnp.bfloat16


def wait_bytes(ref, sem):
    pltpu.make_async_copy(ref, ref, sem).wait()


def iota(shape, dim):
    return lax.broadcasted_iota(jnp.int32, shape, dim)


def kernel(
    n,
    nx,
    total_points,
    x_ref,
    c_ref,
    req_ref,
    out_ref,
    rq,
    onehot,
    onehot_t,
    deal,
    held,
    pick,
    got,
    csq,
    dist,
    resp,
    part,
    back,
    final,
    home,
    w_part,
    w_back,
    w_final,
    w_home,
    gap_own,
    gap_all,
    gap_x,
    send_sem,
    recv_sem,
):
    rp = PAIRS // n
    keys = n * ROWS
    me = lax.axis_index("shard")
    sub = lax.axis_index("sub")

    barrier = pltpu.get_barrier_semaphore()

    def greet(off, carry):
        pl.semaphore_signal(
            barrier, inc=1, device_id=(lax.rem(me + off, n), sub), device_id_type=MESH
        )
        return carry

    lax.fori_loop(1, n, greet, 0)
    for off in range(1, nx):
        pl.semaphore_signal(
            barrier, inc=1, device_id=(me, lax.rem(sub + off, nx)), device_id_type=MESH
        )

    out_row = iota((LANES, LANES), 0)
    in_row = iota((LANES, LANES), 1)
    to_rows = jnp.where(in_row == lax.rem(out_row, ROWS) * OWNED + lax.div(out_row, ROWS), 1.0, 0.0)
    to_pairs = jnp.where(
        out_row == lax.rem(in_row, ROWS) * OWNED + lax.div(in_row, ROWS), 1.0, 0.0
    ).astype(BF16)
    for g in range(PAIRS // 8):
        half = c_ref[:, g * 16 : (g + 1) * 16].astype(BF16).reshape(LANES, NQ * WIDE)
        deal[g * 8 : (g + 1) * 8] = (
            jnp.dot(to_pairs, half, preferred_element_type=F32)
            .astype(BF16)
            .reshape(8, ROWS, NQ * WIDE)
        )

    pl.semaphore_wait(barrier, n - 1 + nx - 1)

    def send(src_of, dst_of, sem):
        def body(off, carry):
            k = lax.rem(me + off, n)
            pltpu.make_async_remote_copy(
                src_ref=src_of(k),
                dst_ref=dst_of(me),
                send_sem=send_sem.at[sem],
                recv_sem=recv_sem.at[sem],
                device_id=(k, sub),
                device_id_type=MESH,
            ).start()
            return carry

        lax.fori_loop(1, n, body, 0)
        pltpu.make_async_copy(src_of(me), dst_of(me), recv_sem.at[sem]).start()

    REQ, GAP, GAP_X, W4, W6, S1 = range(6)
    S3, S4, S6 = (6 + NQ * s for s in range(3))

    def mine(k):
        return pl.ds(k * rp, rp)

    send(lambda k: req_ref, lambda k: rq.at[k], REQ)
    send(lambda k: deal.at[mine(k)], lambda k: held.at[k], S1)

    wait_bytes(rq, recv_sem.at[REQ])

    def build(d, carry):
        here = iota((SLOTS, LANES), 1) == lax.rem(d, 4) * SLOTS + iota((SLOTS, LANES), 0)
        code = jnp.sum(jnp.where(here, rq[d], 0.0), axis=1, keepdims=True)
        for t in range(keys // LANES):
            lane = (iota((SLOTS, LANES), 1) + t * LANES).astype(F32)
            onehot[d, :, t * LANES : (t + 1) * LANES] = jnp.where(code == lane, 1.0, 0.0).astype(BF16)
        return carry

    lax.fori_loop(0, n, build, 0)
    key = iota((keys, LANES), 0).astype(F32)
    for t in range(n // 4):
        code = rq[4 * t] + rq[4 * t + 1] + rq[4 * t + 2] + rq[4 * t + 3]
        onehot_t[:, t * LANES : (t + 1) * LANES] = jnp.where(key == code, 1.0, 0.0).astype(BF16)
    square = jnp.zeros((x_ref.shape[0], LANES), F32)
    for t in range(NQ * WIDE // LANES):
        square = square + jnp.square(x_ref[:, t * LANES : (t + 1) * LANES].astype(F32))
    xsq = lax.dot_general(
        jnp.ones((8, LANES), F32),
        square,
        (((1,), (1,)), ((), ())),
        preferred_element_type=F32,
        precision=lax.Precision.HIGHEST,
    )[:1]

    wait_bytes(held, recv_sem.at[S1])
    some = 8
    for q in range(NQ):
        cols = slice(q * WIDE, (q + 1) * WIDE)

        def select(b, carry):
            here = pl.ds(b * some, some)
            table = onehot[here].reshape(some * SLOTS, keys)
            for r in range(rp):
                chosen = jnp.dot(
                    table, held[:, r, :, cols].reshape(keys, WIDE), preferred_element_type=F32
                )
                pick[q, here, r] = chosen.astype(BF16).reshape(some, SLOTS, WIDE)
            return carry

        lax.fori_loop(0, n // some, select, 0)
        send(lambda k: pick.at[q, k], lambda k: got.at[q, mine(k)], S3 + q)

    step = 16
    stats = []
    for q in range(NQ):
        cols = slice(q * WIDE, (q + 1) * WIDE)
        wait_bytes(got.at[q], recv_sem.at[S3 + q])
        for t in range(NBLK // 2):
            pts = slice(t * 2 * PBLK, (t + 1) * 2 * PBLK)

            def multiply(b, carry):
                here = pl.ds(b * step, step)
                rows = got[q, here, t * 16 : (t + 1) * 16].reshape(step * 16, WIDE)
                dots = lax.dot_general(
                    rows, x_ref[pts, cols], (((1,), (1,)), ((), ())), preferred_element_type=F32
                ).reshape(step, 2, 8, 2 * PBLK)
                wide = jnp.square(rows.astype(F32))
                sq = (wide[:, :LANES] + wide[:, LANES:]).reshape(step, 2, 8, LANES)
                after = []
                for i2 in range(2):
                    i = 2 * t + i2
                    dot = dots[:, i2, :, i2 * PBLK : (i2 + 1) * PBLK]
                    s = sq[:, i2]
                    if q > 0:
                        dot = dist[i, here] + dot
                        s = csq[i, here] + s
                    if q < NQ - 1:
                        dist[i, here] = dot
                        csq[i, here] = s
                    else:
                        x2 = xsq[:, i * PBLK : (i + 1) * PBLK]
                        d = (x2[None] + jnp.sum(s, axis=2, keepdims=True)) - 2.0 * dot
                        dist[i, here] = d
                        after.append(jnp.minimum(carry[2 * i2], jnp.min(d, axis=0)))
                        after.append(carry[2 * i2 + 1] + jnp.sum(d, axis=0))
                return tuple(after)

            start = ()
            if q == NQ - 1:
                start = (jnp.full((8, PBLK), jnp.inf, F32), jnp.zeros((8, PBLK), F32)) * 2
            found = lax.fori_loop(0, PAIRS // step, multiply, start)
            if q == NQ - 1:
                stats += [found[:2], found[2:]]
    least = [jnp.min(m, axis=0, keepdims=True) for m, _ in stats]
    gap = jnp.zeros((1, PBLK), F32)
    for i in range(NBLK):
        gap = gap + (jnp.sum(stats[i][1], axis=0, keepdims=True) / (CAND * CBLK) - least[i])

    gap_own[0] = jnp.broadcast_to(jnp.sum(gap, axis=1, keepdims=True), (1, LANES))
    send(lambda k: gap_own.at[0], lambda k: gap_all.at[k], GAP)
    wait_bytes(gap_all, recv_sem.at[GAP])
    gap_own[1] = jnp.sum(gap_all[...], axis=0)
    gap_x[sub] = gap_own[1]
    for off in range(1, nx):
        pltpu.make_async_remote_copy(
            src_ref=gap_own.at[1],
            dst_ref=gap_x.at[sub],
            send_sem=send_sem.at[GAP_X],
            recv_sem=recv_sem.at[GAP_X],
            device_id=(me, lax.rem(sub + off, nx)),
            device_id_type=MESH,
        ).start()
    if nx > 1:
        wait_bytes(gap_x.at[pl.ds(0, nx - 1)], recv_sem.at[GAP_X])
    spread = jnp.sum(gap_x[...], axis=0)[:, :1] / total_points + 1e-6
    scale = 3.0 / spread

    for i in range(NBLK):

        def exponent(b, norm):
            here = pl.ds(b * step, step)
            e = jnp.exp((least[i][None] - dist[i, here]) * scale[None])
            dist[i, here] = e
            return norm + jnp.sum(e, axis=0)

        norm = lax.fori_loop(0, PAIRS // step, exponent, jnp.zeros((8, PBLK), F32))
        inverse = 1.0 / jnp.sum(norm, axis=0, keepdims=True)

        def normalise(b, carry):
            e = dist[i, pl.ds(b * step, step)]
            resp[i, pl.ds(b * step * 8, step * 8)] = (
                (e * inverse[None]).reshape(step * 8, PBLK).astype(BF16)
            )
            return carry

        lax.fori_loop(0, PAIRS // step, normalise, 0)

    for q in range(NQ):
        cols = slice(q * WIDE, (q + 1) * WIDE)

        def accumulate(b, carry):
            here = pl.ds(b * step * 8, step * 8)
            for t in range(NBLK // 2):
                two = [
                    jnp.dot(
                        resp[i, here],
                        x_ref[i * PBLK : (i + 1) * PBLK, cols],
                        preferred_element_type=F32,
                    ).reshape(step, 8, WIDE)
                    for i in (2 * t, 2 * t + 1)
                ]
                part[q, pl.ds(b * step, step), t * 16 : (t + 1) * 16] = jnp.concatenate(
                    two, axis=1
                ).astype(BF16)
            return carry

        lax.fori_loop(0, PAIRS // step, accumulate, 0)
        send(lambda k: part.at[q, mine(k)], lambda k: back.at[q, k], S4 + q)
    for i in range(NBLK):
        mass = lax.dot_general(
            jnp.ones((8, PBLK), BF16), resp[i], (((1,), (1,)), ((), ())), preferred_element_type=F32
        )[:1]
        mass = mass.astype(BF16).astype(F32)
        for t in range(CAND):
            w_part[t, i] = mass[:, t * LANES : (t + 1) * LANES]
    per_tile = LANES // (8 * rp)
    send(lambda k: w_part.at[lax.div(k, per_tile)], lambda k: w_back.at[k], W4)

    for q in range(NQ):
        wait_bytes(back.at[q], recv_sem.at[S4 + q])

        def combine(b, carry):
            table = onehot_t[pl.ds(b * some * ROWS, some * ROWS)]
            for r in range(rp):
                added = jnp.dot(
                    table, back[q, :, r].reshape(n * SLOTS, WIDE), preferred_element_type=F32
                )
                final[q, pl.ds(b * some, some), r] = added.astype(BF16).reshape(some, ROWS, WIDE)
            return carry

        lax.fori_loop(0, n // some, combine, 0)
        send(lambda k: final.at[q, k], lambda k: home.at[q, mine(k)], S6 + q)
    wait_bytes(w_back, recv_sem.at[W4])
    first = lax.rem(me, per_tile) * 8 * rp
    lane = iota((n, ROWS, LANES), 2)
    row = iota((n, ROWS, LANES), 1)
    weight = jnp.zeros((n, 1, LANES), F32)
    for r in range(rp):
        spot = iota((n, NBLK, 8, LANES), 3) == iota((n, NBLK, 8, LANES), 2) + first + 8 * r
        wide = jnp.where(spot, w_back[...], 0.0).reshape(n * SLOTS, LANES).astype(BF16)
        added = jnp.dot(onehot_t[...], wide, preferred_element_type=F32)
        added = jnp.sum(added, axis=1, keepdims=True).reshape(n, ROWS, 1)
        weight = weight + jnp.sum(
            jnp.where(lane == row + ROWS * r, added, 0.0), axis=1, keepdims=True
        )
    w_final[...] = weight
    send(lambda k: w_final.at[k], lambda k: w_home.at[k], W6)

    wait_bytes(w_home, recv_sem.at[W6])
    for q in range(NQ):
        wait_bytes(home.at[q], recv_sem.at[S6 + q])
    spot = iota((8, ROWS, LANES), 2) == iota((8, ROWS, LANES), 1) + ROWS * lax.rem(
        iota((8, ROWS, LANES), 0), rp
    )
    own = 8 // rp
    for g in range(PAIRS // 8):
        wide = jnp.broadcast_to(w_home[g * own : (g + 1) * own][:, None], (own, rp, 1, LANES))
        wide = jnp.where(spot, wide.reshape(8, 1, LANES), 0.0).reshape(LANES, LANES)
        wide = jnp.dot(
            to_rows, wide, preferred_element_type=F32, precision=lax.Precision.HIGHEST
        )
        inverse = (1.0 / (jnp.sum(wide, axis=1, keepdims=True) + 1.0)).reshape(OWNED, 16, 1)
        for q in range(NQ):
            cols = slice(q * WIDE, (q + 1) * WIDE)
            sums = jnp.dot(
                to_rows.astype(BF16),
                home[q, g * 8 : (g + 1) * 8].reshape(LANES, WIDE),
                preferred_element_type=F32,
            ).reshape(OWNED, 16, WIDE)
            rows = slice(g * 16, (g + 1) * 16)
            out_ref[:, rows, cols] = (sums + 1.0 * c_ref[:, rows, cols]) * inverse

    others = pl.ds(0, n - 1)
    wait_bytes(rq.at[others], send_sem.at[REQ])
    wait_bytes(gap_all.at[others], send_sem.at[GAP])
    if nx > 1:
        wait_bytes(gap_x.at[pl.ds(0, nx - 1)], send_sem.at[GAP_X])
    wait_bytes(w_back.at[others], send_sem.at[W4])
    wait_bytes(w_final.at[others], send_sem.at[W6])
    wait_bytes(held.at[others], send_sem.at[S1])
    for q in range(NQ):
        wait_bytes(pick.at[q, others], send_sem.at[S3 + q])
        wait_bytes(back.at[q, others], send_sem.at[S4 + q])
        wait_bytes(final.at[q, others], send_sem.at[S6 + q])


def on_device(n, nx, points, centroids, cand_peer, cand_block):
    rp = PAIRS // n
    pts, width = points.shape
    code = cand_peer * ROWS + cand_block
    code = code[:, None, :] + OWNED * jnp.arange(2, dtype=jnp.int32)[None, :, None]
    code = jnp.tile(code.reshape(1, SLOTS), (1, LANES // SLOTS))
    place = jnp.arange(LANES, dtype=jnp.int32)[None, :] // SLOTS
    req = jnp.where(place == lax.axis_index("shard") % 4, code, 0).astype(F32)

    vmem = pl.BlockSpec(memory_space=pltpu.VMEM)
    n_sem = 6 + 3 * NQ
    refined = pl.pallas_call(
        functools.partial(kernel, n, nx, pts * n * nx),
        out_shape=jax.ShapeDtypeStruct((OWNED, CBLK, width), F32),
        in_specs=[vmem] * 3,
        out_specs=vmem,
        scratch_shapes=[
            pltpu.VMEM((n, 1, LANES), F32),
            pltpu.VMEM((n, SLOTS, n * ROWS), BF16),
            pltpu.VMEM((n * ROWS, n * SLOTS), BF16),
            pltpu.VMEM((PAIRS, ROWS, width), BF16),
            pltpu.VMEM((n, rp, ROWS, width), BF16),
            pltpu.VMEM((NQ, n, rp, SLOTS, WIDE), BF16),
            pltpu.VMEM((NQ, PAIRS, SLOTS, WIDE), BF16),
            pltpu.VMEM((NBLK, PAIRS, 8, LANES), F32),
            pltpu.VMEM((NBLK, PAIRS, 8, PBLK), F32),
            pltpu.VMEM((NBLK, PAIRS * 8, PBLK), BF16),
            pltpu.VMEM((NQ, PAIRS, SLOTS, WIDE), BF16),
            pltpu.VMEM((NQ, n, rp, SLOTS, WIDE), BF16),
            pltpu.VMEM((NQ, n, rp, ROWS, WIDE), BF16),
            pltpu.VMEM((NQ, PAIRS, ROWS, WIDE), BF16),
            pltpu.VMEM((CAND, NBLK, 1, LANES), F32),
            pltpu.VMEM((n, NBLK, 1, LANES), F32),
            pltpu.VMEM((n, 1, LANES), F32),
            pltpu.VMEM((n, 1, LANES), F32),
            pltpu.VMEM((2, 1, LANES), F32),
            pltpu.VMEM((n, 1, LANES), F32),
            pltpu.VMEM((nx, 1, LANES), F32),
            pltpu.SemaphoreType.DMA((n_sem,)),
            pltpu.SemaphoreType.DMA((n_sem,)),
        ],
        compiler_params=pltpu.CompilerParams(
            collective_id=0, has_side_effects=True, vmem_limit_bytes=VMEM_LIMIT
        ),
    )(points, centroids.reshape(OWNED, CBLK, width), req)
    return refined.reshape(OWNED * CBLK, width)


def solution(mesh):
    placed = P(("shard", "sub"), None)
    body = functools.partial(on_device, mesh.shape["shard"], mesh.shape["sub"])
    return jax.shard_map(
        body, mesh=mesh, in_specs=(placed,) * 4, out_specs=placed, check_vma=False
    )
```

```python
import functools

import jax
import jax.numpy as jnp
from jax import lax
from jax.experimental import pallas as pl
from jax.experimental.pallas import tpu as pltpu
from jax.sharding import PartitionSpec as P

PBLK = 256
CBLK = 128
CAND = 4
NBLK = 4
OWNED = 8
PAIRS = CBLK // 2
ROWS = 2 * OWNED
SLOTS = 2 * NBLK * CAND
NQ = 3
WIDE = 256
LANES = 128
VMEM_LIMIT = 56 * 1024 * 1024
MESH = pl.DeviceIdType.MESH
F32 = jnp.float32
BF16 = jnp.bfloat16


def wait_bytes(ref, sem):
    pltpu.make_async_copy(ref, ref, sem).wait()


def iota(shape, dim):
    return lax.broadcasted_iota(jnp.int32, shape, dim)


def kernel(
    n,
    nx,
    total_points,
    x_hbm,
    c_hbm,
    req_ref,
    out_ref,
    x_ref,
    c_ref,
    rq,
    onehot,
    onehot_t,
    deal,
    held,
    pick,
    got,
    csq,
    dist,
    resp,
    part,
    back,
    final,
    home,
    w_part,
    w_back,
    w_final,
    w_home,
    gap_own,
    gap_lo,
    gap_hi,
    gap_x,
    send_sem,
    recv_sem,
    load_sem,
):
    rp = PAIRS // n
    keys = n * ROWS
    low = gap_lo.shape[0]
    high = n // low
    me = lax.axis_index("shard")
    sub = lax.axis_index("sub")

    load_c = pltpu.make_async_copy(c_hbm, c_ref, load_sem.at[0])
    load_x = pltpu.make_async_copy(x_hbm, x_ref, load_sem.at[1])
    load_c.start()
    load_x.start()

    barrier = pltpu.get_barrier_semaphore()

    def greet(off, carry):
        pl.semaphore_signal(
            barrier, inc=1, device_id=(lax.rem(me + off, n), sub), device_id_type=MESH
        )
        return carry

    lax.fori_loop(1, n, greet, 0, unroll=7)
    for off in range(1, nx):
        pl.semaphore_signal(
            barrier, inc=1, device_id=(me, lax.rem(sub + off, nx)), device_id_type=MESH
        )

    out_row = iota((LANES, LANES), 0)
    in_row = iota((LANES, LANES), 1)
    to_rows = jnp.where(in_row == lax.rem(out_row, ROWS) * OWNED + lax.div(out_row, ROWS), 1.0, 0.0)
    to_pairs = jnp.where(
        out_row == lax.rem(in_row, ROWS) * OWNED + lax.div(in_row, ROWS), 1.0, 0.0
    ).astype(BF16)
    load_c.wait()

    def fill(q):
        for g in range(PAIRS // 8):
            half = c_ref[:, g * 16 : (g + 1) * 16, q * WIDE : (q + 1) * WIDE]
            half = half.astype(BF16).reshape(LANES, WIDE)
            paired = jnp.dot(to_pairs, half, preferred_element_type=F32)
            deal[q, g * 8 : (g + 1) * 8] = paired.astype(BF16).reshape(8, ROWS, WIDE)

    fill(0)
    pl.semaphore_wait(barrier, n - 1 + nx - 1)

    def send(src_of, dst_of, sem):
        def body(off, carry):
            k = lax.rem(me + off, n)
            pltpu.make_async_remote_copy(
                src_ref=src_of(k),
                dst_ref=dst_of(me),
                send_sem=send_sem.at[sem],
                recv_sem=recv_sem.at[sem],
                device_id=(k, sub),
                device_id_type=MESH,
            ).start()
            return carry

        lax.fori_loop(1, n, body, 0, unroll=7)
        pltpu.make_async_copy(src_of(me), dst_of(me), recv_sem.at[sem]).start()

    REQ, GAP_LO, GAP_HI, GAP_X, W4, W6, S1, S1_REST = range(8)
    S3, S4, S6 = (8 + NQ * s for s in range(3))

    def mine(k):
        return pl.ds(k * rp, rp)

    rest = pl.ds(1, NQ - 1)
    send(lambda k: deal.at[0, mine(k)], lambda k: held.at[0, k], S1)
    send(lambda k: req_ref, lambda k: rq.at[k], REQ)
    for q in range(1, NQ):
        fill(q)
    send(lambda k: deal.at[rest, mine(k)], lambda k: held.at[rest, k], S1_REST)

    wait_bytes(rq, recv_sem.at[REQ])

    def build(d, carry):
        here = iota((SLOTS, LANES), 1) == lax.rem(d, 4) * SLOTS + iota((SLOTS, LANES), 0)
        code = jnp.sum(jnp.where(here, rq[d], 0.0), axis=1, keepdims=True)
        for t in range(keys // LANES):
            lane = (iota((SLOTS, LANES), 1) + t * LANES).astype(F32)
            onehot[d, :, t * LANES : (t + 1) * LANES] = jnp.where(code == lane, 1.0, 0.0).astype(BF16)
        return carry

    lax.fori_loop(0, n, build, 0)
    some = 8
    for q in range(NQ):
        if q == 0:
            wait_bytes(held.at[0], recv_sem.at[S1])
        if q == 1:
            wait_bytes(held.at[rest], recv_sem.at[S1_REST])

        def select(b, carry):
            here = pl.ds(b * some, some)
            table = onehot[here].reshape(some * SLOTS, keys)
            for r in range(rp):
                chosen = jnp.dot(
                    table, held[q, :, r].reshape(keys, WIDE), preferred_element_type=F32
                )
                pick[q, here, r] = chosen.astype(BF16).reshape(some, SLOTS, WIDE)
            return carry

        lax.fori_loop(0, n // some, select, 0)
        send(lambda k: pick.at[q, k], lambda k: got.at[q, mine(k)], S3 + q)

    load_x.wait()
    key = iota((keys, LANES), 0).astype(F32)
    for t in range(n // 4):
        code = rq[4 * t] + rq[4 * t + 1] + rq[4 * t + 2] + rq[4 * t + 3]
        onehot_t[:, t * LANES : (t + 1) * LANES] = jnp.where(key == code, 1.0, 0.0).astype(BF16)
    square = jnp.zeros((x_ref.shape[0], LANES), F32)
    for t in range(NQ * WIDE // LANES):
        square = square + jnp.square(x_ref[:, t * LANES : (t + 1) * LANES].astype(F32))
    xsq = lax.dot_general(
        jnp.ones((8, LANES), F32),
        square,
        (((1,), (1,)), ((), ())),
        preferred_element_type=F32,
        precision=lax.Precision.HIGHEST,
    )[:1]

    step = 16
    stats = []
    for q in range(NQ):
        cols = slice(q * WIDE, (q + 1) * WIDE)
        wait_bytes(got.at[q], recv_sem.at[S3 + q])
        for t in range(NBLK // 2):
            pts = slice(t * 2 * PBLK, (t + 1) * 2 * PBLK)

            def multiply(b, carry):
                here = pl.ds(b * step, step)
                rows = got[q, here, t * 16 : (t + 1) * 16].reshape(step * 16, WIDE)
                dots = lax.dot_general(
                    rows, x_ref[pts, cols], (((1,), (1,)), ((), ())), preferred_element_type=F32
                ).reshape(step, 2, 8, 2 * PBLK)
                wide = jnp.square(rows.astype(F32))
                sq = (wide[:, :LANES] + wide[:, LANES:]).reshape(step, 2, 8, LANES)
                after = []
                for i2 in range(2):
                    i = 2 * t + i2
                    dot = dots[:, i2, :, i2 * PBLK : (i2 + 1) * PBLK]
                    s = sq[:, i2]
                    if q > 0:
                        dot = dist[i, here] + dot
                        s = csq[i, here] + s
                    if q < NQ - 1:
                        dist[i, here] = dot
                        csq[i, here] = s
                    else:
                        x2 = xsq[:, i * PBLK : (i + 1) * PBLK]
                        d = (x2[None] + jnp.sum(s, axis=2, keepdims=True)) - 2.0 * dot
                        dist[i, here] = d
                        after.append(jnp.minimum(carry[2 * i2], jnp.min(d, axis=0)))
                        after.append(carry[2 * i2 + 1] + jnp.sum(d, axis=0))
                return tuple(after)

            start = ()
            if q == NQ - 1:
                start = (jnp.full((8, PBLK), jnp.inf, F32), jnp.zeros((8, PBLK), F32)) * 2
            found = lax.fori_loop(0, PAIRS // step, multiply, start)
            if q == NQ - 1:
                stats += [found[:2], found[2:]]
    least = [jnp.min(m, axis=0, keepdims=True) for m, _ in stats]
    gap = jnp.zeros((1, PBLK), F32)
    for i in range(NBLK):
        gap = gap + (jnp.sum(stats[i][1], axis=0, keepdims=True) / (CAND * CBLK) - least[i])

    gap_own[0] = jnp.broadcast_to(jnp.sum(gap, axis=1, keepdims=True), (1, LANES))
    lo = lax.rem(me, low)
    hi = lax.div(me, low)

    def share(of, into, at, devices, sem):
        into[at] = gap_own[of]
        for device in devices:
            pltpu.make_async_remote_copy(
                src_ref=gap_own.at[of],
                dst_ref=into.at[at],
                send_sem=send_sem.at[sem],
                recv_sem=recv_sem.at[sem],
                device_id=device,
                device_id_type=MESH,
            ).start()
        if devices:
            wait_bytes(into.at[pl.ds(0, len(devices))], recv_sem.at[sem])
        return jnp.sum(into[...], axis=0)

    gap_own[1] = share(
        0, gap_lo, lo, [(hi * low + lax.rem(lo + o, low), sub) for o in range(1, low)], GAP_LO
    )
    gap_own[2] = share(
        1, gap_hi, hi, [(lax.rem(hi + o, high) * low + lo, sub) for o in range(1, high)], GAP_HI
    )
    every = share(2, gap_x, sub, [(me, lax.rem(sub + o, nx)) for o in range(1, nx)], GAP_X)
    spread = every[:, :1] / total_points + 1e-6
    scale = 3.0 / spread

    for i in range(NBLK):

        def exponent(b, norm):
            here = pl.ds(b * step, step)
            e = jnp.exp((least[i][None] - dist[i, here]) * scale[None])
            dist[i, here] = e
            return norm + jnp.sum(e, axis=0)

        norm = lax.fori_loop(0, PAIRS // step, exponent, jnp.zeros((8, PBLK), F32))
        inverse = 1.0 / jnp.sum(norm, axis=0, keepdims=True)

        def normalise(b, carry):
            e = dist[i, pl.ds(b * step, step)]
            resp[i, pl.ds(b * step * 8, step * 8)] = (
                (e * inverse[None]).reshape(step * 8, PBLK).astype(BF16)
            )
            return carry

        lax.fori_loop(0, PAIRS // step, normalise, 0)

    per_tile = LANES // (8 * rp)

    for q in range(NQ):
        cols = slice(q * WIDE, (q + 1) * WIDE)

        def accumulate(b, carry):
            here = pl.ds(b * step * 8, step * 8)
            for t in range(NBLK // 2):
                two = [
                    jnp.dot(
                        resp[i, here],
                        x_ref[i * PBLK : (i + 1) * PBLK, cols],
                        preferred_element_type=F32,
                    ).reshape(step, 8, WIDE)
                    for i in (2 * t, 2 * t + 1)
                ]
                part[q, pl.ds(b * step, step), t * 16 : (t + 1) * 16] = jnp.concatenate(
                    two, axis=1
                ).astype(BF16)
            return carry

        lax.fori_loop(0, PAIRS // step, accumulate, 0)
        send(lambda k: part.at[q, mine(k)], lambda k: back.at[q, k], S4 + q)
        if q == 0:
            for i in range(NBLK):
                mass = lax.dot_general(
                    jnp.ones((8, PBLK), BF16), resp[i], (((1,), (1,)), ((), ())), preferred_element_type=F32
                )[:1]
                mass = mass.astype(BF16).astype(F32)
                for t in range(CAND):
                    w_part[t, i] = mass[:, t * LANES : (t + 1) * LANES]
            send(lambda k: w_part.at[lax.div(k, per_tile)], lambda k: w_back.at[k], W4)

    for q in range(NQ):
        wait_bytes(back.at[q], recv_sem.at[S4 + q])

        def combine(b, carry):
            table = onehot_t[pl.ds(b * some * ROWS, some * ROWS)]
            for r in range(rp):
                added = jnp.dot(
                    table, back[q, :, r].reshape(n * SLOTS, WIDE), preferred_element_type=F32
                )
                final[q, pl.ds(b * some, some), r] = added.astype(BF16).reshape(some, ROWS, WIDE)
            return carry

        lax.fori_loop(0, n // some, combine, 0)
        send(lambda k: final.at[q, k], lambda k: home.at[q, mine(k)], S6 + q)
        if q == 0:
            wait_bytes(w_back, recv_sem.at[W4])
            first = lax.rem(me, per_tile) * 8 * rp
            lane = iota((n, ROWS, LANES), 2)
            row = iota((n, ROWS, LANES), 1)
            weight = jnp.zeros((n, 1, LANES), F32)
            for r in range(rp):
                spot = iota((n, NBLK, 8, LANES), 3) == iota((n, NBLK, 8, LANES), 2) + first + 8 * r
                wide = jnp.where(spot, w_back[...], 0.0).reshape(n * SLOTS, LANES).astype(BF16)
                added = jnp.dot(onehot_t[...], wide, preferred_element_type=F32)
                added = jnp.sum(added, axis=1, keepdims=True).reshape(n, ROWS, 1)
                weight = weight + jnp.sum(
                    jnp.where(lane == row + ROWS * r, added, 0.0), axis=1, keepdims=True
                )
            w_final[...] = weight
            send(lambda k: w_final.at[k], lambda k: w_home.at[k], W6)

    wait_bytes(w_home, recv_sem.at[W6])
    spot = iota((8, ROWS, LANES), 2) == iota((8, ROWS, LANES), 1) + ROWS * lax.rem(
        iota((8, ROWS, LANES), 0), rp
    )
    own = 8 // rp
    inverse = []
    for g in range(PAIRS // 8):
        wide = jnp.broadcast_to(w_home[g * own : (g + 1) * own][:, None], (own, rp, 1, LANES))
        wide = jnp.where(spot, wide.reshape(8, 1, LANES), 0.0).reshape(LANES, LANES)
        wide = jnp.dot(
            to_rows, wide, preferred_element_type=F32, precision=lax.Precision.HIGHEST
        )
        wide = 1.0 / (jnp.sum(wide, axis=1, keepdims=True) + 1.0)
        inverse.append(wide.reshape(OWNED, 16, 1))
    for q in range(NQ):
        cols = slice(q * WIDE, (q + 1) * WIDE)
        wait_bytes(home.at[q], recv_sem.at[S6 + q])
        for g in range(PAIRS // 8):
            sums = jnp.dot(
                to_rows.astype(BF16),
                home[q, g * 8 : (g + 1) * 8].reshape(LANES, WIDE),
                preferred_element_type=F32,
            ).reshape(OWNED, 16, WIDE)
            rows = slice(g * 16, (g + 1) * 16)
            out_ref[:, rows, cols] = (sums + 1.0 * c_ref[:, rows, cols]) * inverse[g]

    others = pl.ds(0, n - 1)
    wait_bytes(rq.at[others], send_sem.at[REQ])
    wait_bytes(gap_lo.at[pl.ds(0, low - 1)], send_sem.at[GAP_LO])
    wait_bytes(gap_hi.at[pl.ds(0, high - 1)], send_sem.at[GAP_HI])
    if nx > 1:
        wait_bytes(gap_x.at[pl.ds(0, nx - 1)], send_sem.at[GAP_X])
    wait_bytes(w_back.at[others], send_sem.at[W4])
    wait_bytes(w_final.at[others], send_sem.at[W6])
    wait_bytes(held.at[0, others], send_sem.at[S1])
    wait_bytes(held.at[rest, others], send_sem.at[S1_REST])
    for q in range(NQ):
        wait_bytes(pick.at[q, others], send_sem.at[S3 + q])
        wait_bytes(back.at[q, others], send_sem.at[S4 + q])
        wait_bytes(final.at[q, others], send_sem.at[S6 + q])


def on_device(n, nx, points, centroids, cand_peer, cand_block):
    rp = PAIRS // n
    pts, width = points.shape
    code = cand_peer * ROWS + cand_block
    code = code[:, None, :] + OWNED * jnp.arange(2, dtype=jnp.int32)[None, :, None]
    code = jnp.tile(code.reshape(1, SLOTS), (1, LANES // SLOTS))
    place = jnp.arange(LANES, dtype=jnp.int32)[None, :] // SLOTS
    req = jnp.where(place == lax.axis_index("shard") % 4, code, 0).astype(F32)

    vmem = pl.BlockSpec(memory_space=pltpu.VMEM)
    n_sem = 8 + 3 * NQ
    low = 8 if n >= 64 else 4
    hbm = pl.BlockSpec(memory_space=pl.ANY)
    refined = pl.pallas_call(
        functools.partial(kernel, n, nx, pts * n * nx),
        out_shape=jax.ShapeDtypeStruct((OWNED, CBLK, width), F32),
        in_specs=[hbm, hbm, vmem],
        out_specs=vmem,
        scratch_shapes=[
            pltpu.VMEM((pts, width), BF16),
            pltpu.VMEM((OWNED, CBLK, width), F32),
            pltpu.VMEM((n, 1, LANES), F32),
            pltpu.VMEM((n, SLOTS, n * ROWS), BF16),
            pltpu.VMEM((n * ROWS, n * SLOTS), BF16),
            pltpu.VMEM((NQ, PAIRS, ROWS, WIDE), BF16),
            pltpu.VMEM((NQ, n, rp, ROWS, WIDE), BF16),
            pltpu.VMEM((NQ, n, rp, SLOTS, WIDE), BF16),
            pltpu.VMEM((NQ, PAIRS, SLOTS, WIDE), BF16),
            pltpu.VMEM((NBLK, PAIRS, 8, LANES), F32),
            pltpu.VMEM((NBLK, PAIRS, 8, PBLK), F32),
            pltpu.VMEM((NBLK, PAIRS * 8, PBLK), BF16),
            pltpu.VMEM((NQ, PAIRS, SLOTS, WIDE), BF16),
            pltpu.VMEM((NQ, n, rp, SLOTS, WIDE), BF16),
            pltpu.VMEM((NQ, n, rp, ROWS, WIDE), BF16),
            pltpu.VMEM((NQ, PAIRS, ROWS, WIDE), BF16),
            pltpu.VMEM((CAND, NBLK, 1, LANES), F32),
            pltpu.VMEM((n, NBLK, 1, LANES), F32),
            pltpu.VMEM((n, 1, LANES), F32),
            pltpu.VMEM((n, 1, LANES), F32),
            pltpu.VMEM((3, 1, LANES), F32),
            pltpu.VMEM((low, 1, LANES), F32),
            pltpu.VMEM((n // low, 1, LANES), F32),
            pltpu.VMEM((nx, 1, LANES), F32),
            pltpu.SemaphoreType.DMA((n_sem,)),
            pltpu.SemaphoreType.DMA((n_sem,)),
            pltpu.SemaphoreType.DMA((2,)),
        ],
        compiler_params=pltpu.CompilerParams(
            collective_id=0, has_side_effects=True, vmem_limit_bytes=VMEM_LIMIT
        ),
    )(points, centroids.reshape(OWNED, CBLK, width), req)
    return refined.reshape(OWNED * CBLK, width)


def solution(mesh):
    placed = P(("shard", "sub"), None)
    body = functools.partial(on_device, mesh.shape["shard"], mesh.shape["sub"])
    return jax.shard_map(
        body, mesh=mesh, in_specs=(placed,) * 4, out_specs=placed, check_vma=False
    )
```

```python
import functools

import jax
import jax.numpy as jnp
from jax import lax
from jax.experimental import pallas as pl
from jax.experimental.pallas import tpu as pltpu
from jax.sharding import PartitionSpec as P

PBLK = 256
CBLK = 128
CAND = 4
NBLK = 4
OWNED = 8
PAIRS = CBLK // 2
ROWS = 2 * OWNED
SLOTS = 2 * NBLK * CAND
NQ = 3
WIDE = 256
LANES = 128
VMEM_LIMIT = 56 * 1024 * 1024
MESH = pl.DeviceIdType.MESH
F32 = jnp.float32
BF16 = jnp.bfloat16


def wait_bytes(ref, sem):
    pltpu.make_async_copy(ref, ref, sem).wait()


def iota(shape, dim):
    return lax.broadcasted_iota(jnp.int32, shape, dim)


def kernel(
    n,
    nx,
    total_points,
    x_hbm,
    c_hbm,
    peer_ref,
    block_ref,
    out_hbm,
    req_ref,
    out_ref,
    x_ref,
    c_ref,
    rq,
    onehot,
    onehot_t,
    deal,
    held,
    pick,
    got,
    csq,
    dist,
    resp,
    part,
    back,
    final,
    home,
    w_part,
    w_back,
    w_final,
    w_home,
    gap_own,
    gap_lo,
    gap_hi,
    send_sem,
    recv_sem,
    load_sem,
    out_sem,
):
    rp = PAIRS // n
    keys = n * ROWS
    low = gap_lo.shape[0]
    high = n // low
    me = lax.axis_index("shard")
    sub = lax.axis_index("sub")
    lo = lax.rem(me, low)
    hi = lax.div(me, low)

    load_c = pltpu.make_async_copy(c_hbm, c_ref, load_sem.at[0])
    load_x = pltpu.make_async_copy(x_hbm, x_ref, load_sem.at[1])
    load_c.start()
    load_x.start()

    barrier = pltpu.get_barrier_semaphore()

    def greet(off, carry):
        pl.semaphore_signal(
            barrier, inc=1, device_id=(lax.rem(me + off, n), sub), device_id_type=MESH
        )
        return carry

    lax.fori_loop(1, n, greet, 0, unroll=7)
    for off in range(1, nx):
        for up in range(high):
            other = (lax.rem(hi + up, high) * low + lo, lax.rem(sub + off, nx))
            pl.semaphore_signal(barrier, inc=1, device_id=other, device_id_type=MESH)

    out_row = iota((LANES, LANES), 0)
    in_row = iota((LANES, LANES), 1)
    to_rows = jnp.where(in_row == lax.rem(out_row, ROWS) * OWNED + lax.div(out_row, ROWS), 1.0, 0.0)
    to_pairs = jnp.where(
        out_row == lax.rem(in_row, ROWS) * OWNED + lax.div(in_row, ROWS), 1.0, 0.0
    ).astype(BF16)
    load_c.wait()

    def fill(q):
        for g in range(PAIRS // 8):
            half = c_ref[:, g * 16 : (g + 1) * 16, q * WIDE : (q + 1) * WIDE]
            half = half.astype(BF16).reshape(LANES, WIDE)
            paired = jnp.dot(to_pairs, half, preferred_element_type=F32)
            deal[q, g * 8 : (g + 1) * 8] = paired.astype(BF16).reshape(8, ROWS, WIDE)

    fill(0)
    lane = iota((1, LANES), 1)
    code = jnp.zeros((1, LANES), jnp.int32)
    for i in range(NBLK):
        for j in range(CAND):
            here = lax.rem(lane, SLOTS)
            here = (lax.div(here, 2 * CAND) == i) & (lax.rem(here, CAND) == j)
            code = jnp.where(here, peer_ref[i, j] * ROWS + block_ref[i, j], code)
    code = code + OWNED * lax.rem(lax.div(lane, CAND), 2)
    req_ref[...] = jnp.where(lax.div(lane, SLOTS) == lax.rem(me, 4), code, 0).astype(F32)

    pl.semaphore_wait(barrier, n - 1 + (nx - 1) * high)

    def send(src_of, dst_of, sem):
        def body(off, carry):
            k = lax.rem(me + off, n)
            pltpu.make_async_remote_copy(
                src_ref=src_of(k),
                dst_ref=dst_of(me),
                send_sem=send_sem.at[sem],
                recv_sem=recv_sem.at[sem],
                device_id=(k, sub),
                device_id_type=MESH,
            ).start()
            return carry

        lax.fori_loop(1, n, body, 0, unroll=7)
        pltpu.make_async_copy(src_of(me), dst_of(me), recv_sem.at[sem]).start()

    REQ, GAP_LO, GAP_HI, W4, W6, S1, S1_REST = range(7)
    S3, S4, S6 = (7 + NQ * s for s in range(3))

    def mine(k):
        return pl.ds(k * rp, rp)

    rest = pl.ds(1, NQ - 1)
    send(lambda k: deal.at[0, mine(k)], lambda k: held.at[0, k], S1)
    send(lambda k: req_ref, lambda k: rq.at[k], REQ)
    for q in range(1, NQ):
        fill(q)
    send(lambda k: deal.at[rest, mine(k)], lambda k: held.at[rest, k], S1_REST)

    wait_bytes(rq, recv_sem.at[REQ])

    def build(d, carry):
        here = iota((SLOTS, LANES), 1) == lax.rem(d, 4) * SLOTS + iota((SLOTS, LANES), 0)
        code = jnp.sum(jnp.where(here, rq[d], 0.0), axis=1, keepdims=True)
        for t in range(keys // LANES):
            lane = (iota((SLOTS, LANES), 1) + t * LANES).astype(F32)
            onehot[d, :, t * LANES : (t + 1) * LANES] = jnp.where(code == lane, 1.0, 0.0).astype(BF16)
        return carry

    lax.fori_loop(0, n, build, 0)
    some = 8
    for q in range(NQ):
        if q == 0:
            wait_bytes(held.at[0], recv_sem.at[S1])
        if q == 1:
            wait_bytes(held.at[rest], recv_sem.at[S1_REST])

        def select(b, carry):
            here = pl.ds(b * some, some)
            table = onehot[here].reshape(some * SLOTS, keys)
            for r in range(rp):
                chosen = jnp.dot(
                    table, held[q, :, r].reshape(keys, WIDE), preferred_element_type=F32
                )
                pick[q, here, r] = chosen.astype(BF16).reshape(some, SLOTS, WIDE)
            return carry

        lax.fori_loop(0, n // some, select, 0)
        send(lambda k: pick.at[q, k], lambda k: got.at[q, mine(k)], S3 + q)

    load_x.wait()
    key = iota((keys, LANES), 0).astype(F32)
    for t in range(n // 4):
        code = rq[4 * t] + rq[4 * t + 1] + rq[4 * t + 2] + rq[4 * t + 3]
        onehot_t[:, t * LANES : (t + 1) * LANES] = jnp.where(key == code, 1.0, 0.0).astype(BF16)
    square = jnp.zeros((x_ref.shape[0], LANES), F32)
    for t in range(NQ * WIDE // LANES):
        square = square + jnp.square(x_ref[:, t * LANES : (t + 1) * LANES].astype(F32))
    xsq = lax.dot_general(
        jnp.ones((8, LANES), F32),
        square,
        (((1,), (1,)), ((), ())),
        preferred_element_type=F32,
        precision=lax.Precision.HIGHEST,
    )[:1]

    step = 16
    stats = []
    for q in range(NQ):
        cols = slice(q * WIDE, (q + 1) * WIDE)
        wait_bytes(got.at[q], recv_sem.at[S3 + q])
        for t in range(NBLK // 2):
            pts = slice(t * 2 * PBLK, (t + 1) * 2 * PBLK)

            def multiply(b, carry):
                here = pl.ds(b * step, step)
                rows = got[q, here, t * 16 : (t + 1) * 16].reshape(step * 16, WIDE)
                dots = lax.dot_general(
                    rows, x_ref[pts, cols], (((1,), (1,)), ((), ())), preferred_element_type=F32
                ).reshape(step, 2, 8, 2 * PBLK)
                wide = jnp.square(rows.astype(F32))
                sq = (wide[:, :LANES] + wide[:, LANES:]).reshape(step, 2, 8, LANES)
                after = []
                for i2 in range(2):
                    i = 2 * t + i2
                    dot = dots[:, i2, :, i2 * PBLK : (i2 + 1) * PBLK]
                    s = sq[:, i2]
                    if q > 0:
                        dot = dist[i, here] + dot
                        s = csq[i, here] + s
                    if q < NQ - 1:
                        dist[i, here] = dot
                        csq[i, here] = s
                    else:
                        x2 = xsq[:, i * PBLK : (i + 1) * PBLK]
                        d = (x2[None] + jnp.sum(s, axis=2, keepdims=True)) - 2.0 * dot
                        dist[i, here] = d
                        after.append(jnp.minimum(carry[2 * i2], jnp.min(d, axis=0)))
                        after.append(carry[2 * i2 + 1] + jnp.sum(d, axis=0))
                return tuple(after)

            start = ()
            if q == NQ - 1:
                start = (jnp.full((8, PBLK), jnp.inf, F32), jnp.zeros((8, PBLK), F32)) * 2
            found = lax.fori_loop(0, PAIRS // step, multiply, start)
            if q == NQ - 1:
                stats += [found[:2], found[2:]]
    least = [jnp.min(m, axis=0, keepdims=True) for m, _ in stats]
    gap = jnp.zeros((1, PBLK), F32)
    for i in range(NBLK):
        gap = gap + (jnp.sum(stats[i][1], axis=0, keepdims=True) / (CAND * CBLK) - least[i])

    gap_own[0] = jnp.broadcast_to(jnp.sum(gap, axis=1, keepdims=True), (1, LANES))

    def share(of, into, at, devices, sem):
        into[at] = gap_own[of]
        for device in devices:
            pltpu.make_async_remote_copy(
                src_ref=gap_own.at[of],
                dst_ref=into.at[at],
                send_sem=send_sem.at[sem],
                recv_sem=recv_sem.at[sem],
                device_id=device,
                device_id_type=MESH,
            ).start()
        if len(devices) > 0:
            wait_bytes(into.at[pl.ds(0, len(devices))], recv_sem.at[sem])
        return jnp.sum(into[...], axis=0)

    gap_own[1] = share(
        0, gap_lo, lo, [(hi * low + lax.rem(lo + o, low), sub) for o in range(1, low)], GAP_LO
    )
    across = high * nx
    place = hi * nx + sub
    others = [lax.rem(place + o, across) for o in range(1, across)]
    others = [(lax.div(o, nx) * low + lo, lax.rem(o, nx)) for o in others]
    every = share(1, gap_hi, place, others, GAP_HI)
    spread = every[:, :1] / total_points + 1e-6
    scale = 3.0 / spread

    for i in range(NBLK):

        def exponent(b, norm):
            here = pl.ds(b * step, step)
            e = jnp.exp((least[i][None] - dist[i, here]) * scale[None])
            dist[i, here] = e
            return norm + jnp.sum(e, axis=0)

        norm = lax.fori_loop(0, PAIRS // step, exponent, jnp.zeros((8, PBLK), F32))
        inverse = 1.0 / jnp.sum(norm, axis=0, keepdims=True)

        def normalise(b, carry):
            e = dist[i, pl.ds(b * step, step)]
            resp[i, pl.ds(b * step * 8, step * 8)] = (
                (e * inverse[None]).reshape(step * 8, PBLK).astype(BF16)
            )
            return carry

        lax.fori_loop(0, PAIRS // step, normalise, 0)

    per_tile = LANES // (8 * rp)

    for q in range(NQ):
        cols = slice(q * WIDE, (q + 1) * WIDE)

        def accumulate(b, carry):
            here = pl.ds(b * step * 8, step * 8)
            for t in range(NBLK // 2):
                two = [
                    jnp.dot(
                        resp[i, here],
                        x_ref[i * PBLK : (i + 1) * PBLK, cols],
                        preferred_element_type=F32,
                    ).reshape(step, 8, WIDE)
                    for i in (2 * t, 2 * t + 1)
                ]
                part[q, pl.ds(b * step, step), t * 16 : (t + 1) * 16] = jnp.concatenate(
                    two, axis=1
                ).astype(BF16)
            return carry

        lax.fori_loop(0, PAIRS // step, accumulate, 0)
        send(lambda k: part.at[q, mine(k)], lambda k: back.at[q, k], S4 + q)
        if q == 0:
            for i in range(NBLK):
                mass = lax.dot_general(
                    jnp.ones((8, PBLK), BF16), resp[i], (((1,), (1,)), ((), ())), preferred_element_type=F32
                )[:1]
                mass = mass.astype(BF16).astype(F32)
                for t in range(CAND):
                    w_part[t, i] = mass[:, t * LANES : (t + 1) * LANES]
            send(lambda k: w_part.at[lax.div(k, per_tile)], lambda k: w_back.at[k], W4)

    for q in range(NQ):
        wait_bytes(back.at[q], recv_sem.at[S4 + q])

        def combine(b, carry):
            table = onehot_t[pl.ds(b * some * ROWS, some * ROWS)]
            for r in range(rp):
                added = jnp.dot(
                    table, back[q, :, r].reshape(n * SLOTS, WIDE), preferred_element_type=F32
                )
                final[q, pl.ds(b * some, some), r] = added.astype(BF16).reshape(some, ROWS, WIDE)
            return carry

        lax.fori_loop(0, n // some, combine, 0)
        send(lambda k: final.at[q, k], lambda k: home.at[q, mine(k)], S6 + q)
        if q == 0:
            wait_bytes(w_back, recv_sem.at[W4])
            first = lax.rem(me, per_tile) * 8 * rp
            lane = iota((n, ROWS, LANES), 2)
            row = iota((n, ROWS, LANES), 1)
            weight = jnp.zeros((n, 1, LANES), F32)
            for r in range(rp):
                spot = iota((n, NBLK, 8, LANES), 3) == iota((n, NBLK, 8, LANES), 2) + first + 8 * r
                wide = jnp.where(spot, w_back[...], 0.0).reshape(n * SLOTS, LANES).astype(BF16)
                added = jnp.dot(onehot_t[...], wide, preferred_element_type=F32)
                added = jnp.sum(added, axis=1, keepdims=True).reshape(n, ROWS, 1)
                weight = weight + jnp.sum(
                    jnp.where(lane == row + ROWS * r, added, 0.0), axis=1, keepdims=True
                )
            w_final[...] = weight
            send(lambda k: w_final.at[k], lambda k: w_home.at[k], W6)

    wait_bytes(w_home, recv_sem.at[W6])
    spot = iota((8, ROWS, LANES), 2) == iota((8, ROWS, LANES), 1) + ROWS * lax.rem(
        iota((8, ROWS, LANES), 0), rp
    )
    own = 8 // rp
    inverse = []
    for g in range(PAIRS // 8):
        wide = jnp.broadcast_to(w_home[g * own : (g + 1) * own][:, None], (own, rp, 1, LANES))
        wide = jnp.where(spot, wide.reshape(8, 1, LANES), 0.0).reshape(LANES, LANES)
        wide = jnp.dot(
            to_rows, wide, preferred_element_type=F32, precision=lax.Precision.HIGHEST
        )
        wide = 1.0 / (jnp.sum(wide, axis=1, keepdims=True) + 1.0)
        inverse.append(wide.reshape(OWNED, 16, 1))
    for q in range(NQ):
        cols = slice(q * WIDE, (q + 1) * WIDE)
        wait_bytes(home.at[q], recv_sem.at[S6 + q])
        for g in range(PAIRS // 8):
            sums = jnp.dot(
                to_rows.astype(BF16),
                home[q, g * 8 : (g + 1) * 8].reshape(LANES, WIDE),
                preferred_element_type=F32,
            ).reshape(OWNED, 16, WIDE)
            rows = slice(g * 16, (g + 1) * 16)
            out_ref[:, rows, cols] = (sums + 1.0 * c_ref[:, rows, cols]) * inverse[g]
        pltpu.make_async_copy(
            out_ref.at[:, :, cols], out_hbm.at[:, :, cols], out_sem.at[q]
        ).start()

    others = pl.ds(0, n - 1)
    wait_bytes(rq.at[others], send_sem.at[REQ])
    wait_bytes(gap_lo.at[pl.ds(0, low - 1)], send_sem.at[GAP_LO])
    wait_bytes(gap_hi.at[pl.ds(0, across - 1)], send_sem.at[GAP_HI])
    wait_bytes(w_back.at[others], send_sem.at[W4])
    wait_bytes(w_final.at[others], send_sem.at[W6])
    wait_bytes(held.at[0, others], send_sem.at[S1])
    wait_bytes(held.at[rest, others], send_sem.at[S1_REST])
    for q in range(NQ):
        wait_bytes(pick.at[q, others], send_sem.at[S3 + q])
        wait_bytes(back.at[q, others], send_sem.at[S4 + q])
        wait_bytes(final.at[q, others], send_sem.at[S6 + q])
    for q in range(NQ):
        cols = slice(q * WIDE, (q + 1) * WIDE)
        pltpu.make_async_copy(
            out_ref.at[:, :, cols], out_hbm.at[:, :, cols], out_sem.at[q]
        ).wait()


def on_device(n, nx, points, centroids, cand_peer, cand_block):
    rp = PAIRS // n
    pts, width = points.shape
    smem = pl.BlockSpec(memory_space=pltpu.SMEM)
    n_sem = 7 + 3 * NQ
    low = 16 if n >= 64 else 4
    hbm = pl.BlockSpec(memory_space=pl.ANY)
    refined = pl.pallas_call(
        functools.partial(kernel, n, nx, pts * n * nx),
        out_shape=jax.ShapeDtypeStruct((OWNED, CBLK, width), F32),
        in_specs=[hbm, hbm, smem, smem],
        out_specs=hbm,
        scratch_shapes=[
            pltpu.VMEM((1, LANES), F32),
            pltpu.VMEM((OWNED, CBLK, width), F32),
            pltpu.VMEM((pts, width), BF16),
            pltpu.VMEM((OWNED, CBLK, width), F32),
            pltpu.VMEM((n, 1, LANES), F32),
            pltpu.VMEM((n, SLOTS, n * ROWS), BF16),
            pltpu.VMEM((n * ROWS, n * SLOTS), BF16),
            pltpu.VMEM((NQ, PAIRS, ROWS, WIDE), BF16),
            pltpu.VMEM((NQ, n, rp, ROWS, WIDE), BF16),
            pltpu.VMEM((NQ, n, rp, SLOTS, WIDE), BF16),
            pltpu.VMEM((NQ, PAIRS, SLOTS, WIDE), BF16),
            pltpu.VMEM((NBLK, PAIRS, 8, LANES), F32),
            pltpu.VMEM((NBLK, PAIRS, 8, PBLK), F32),
            pltpu.VMEM((NBLK, PAIRS * 8, PBLK), BF16),
            pltpu.VMEM((NQ, PAIRS, SLOTS, WIDE), BF16),
            pltpu.VMEM((NQ, n, rp, SLOTS, WIDE), BF16),
            pltpu.VMEM((NQ, n, rp, ROWS, WIDE), BF16),
            pltpu.VMEM((NQ, PAIRS, ROWS, WIDE), BF16),
            pltpu.VMEM((CAND, NBLK, 1, LANES), F32),
            pltpu.VMEM((n, NBLK, 1, LANES), F32),
            pltpu.VMEM((n, 1, LANES), F32),
            pltpu.VMEM((n, 1, LANES), F32),
            pltpu.VMEM((2, 1, LANES), F32),
            pltpu.VMEM((low, 1, LANES), F32),
            pltpu.VMEM((n // low * nx, 1, LANES), F32),
            pltpu.SemaphoreType.DMA((n_sem,)),
            pltpu.SemaphoreType.DMA((n_sem,)),
            pltpu.SemaphoreType.DMA((2,)),
            pltpu.SemaphoreType.DMA((NQ,)),
        ],
        compiler_params=pltpu.CompilerParams(
            collective_id=0, has_side_effects=True, vmem_limit_bytes=VMEM_LIMIT
        ),
    )(points, centroids.reshape(OWNED, CBLK, width), cand_peer, cand_block)
    return refined.reshape(OWNED * CBLK, width)


def solution(mesh):
    placed = P(("shard", "sub"), None)
    body = functools.partial(on_device, mesh.shape["shard"], mesh.shape["sub"])
    return jax.shard_map(
        body, mesh=mesh, in_specs=(placed,) * 4, out_specs=placed, check_vma=False
    )
```

```python
import functools

import jax
import jax.numpy as jnp
from jax import lax
from jax.experimental import pallas as pl
from jax.experimental.pallas import tpu as pltpu
from jax.sharding import PartitionSpec as P

PBLK = 256
CBLK = 128
CAND = 4
NBLK = 4
OWNED = 8
PAIRS = CBLK // 2
ROWS = 2 * OWNED
SLOTS = 2 * NBLK * CAND
NQ = 3
WIDE = 256
LANES = 128
VMEM_LIMIT = 56 * 1024 * 1024
MESH = pl.DeviceIdType.MESH
F32 = jnp.float32
BF16 = jnp.bfloat16


def wait_bytes(ref, sem):
    pltpu.make_async_copy(ref, ref, sem).wait()


def iota(shape, dim):
    return lax.broadcasted_iota(jnp.int32, shape, dim)


def kernel(
    n,
    nx,
    total_points,
    x_hbm,
    c_hbm,
    peer_ref,
    block_ref,
    out_hbm,
    req_ref,
    out_ref,
    x_ref,
    c_ref,
    rq,
    onehot,
    onehot_t,
    deal,
    held,
    pick,
    got,
    csq,
    dist,
    resp,
    pack,
    part,
    back,
    final,
    home,
    w_part,
    w_back,
    w_final,
    w_home,
    gap_own,
    gap_lo,
    gap_hi,
    send_sem,
    recv_sem,
    load_sem,
    out_sem,
):
    rp = PAIRS // n
    keys = n * ROWS
    low = gap_lo.shape[0]
    high = n // low
    me = lax.axis_index("shard")
    sub = lax.axis_index("sub")
    lo = lax.rem(me, low)
    hi = lax.div(me, low)

    load_c = pltpu.make_async_copy(c_hbm, c_ref, load_sem.at[0])
    load_x = pltpu.make_async_copy(x_hbm, x_ref, load_sem.at[1])
    load_c.start()
    load_x.start()

    barrier = pltpu.get_barrier_semaphore()

    def greet(off, carry):
        pl.semaphore_signal(
            barrier, inc=1, device_id=(lax.rem(me + off, n), sub), device_id_type=MESH
        )
        return carry

    lax.fori_loop(1, n, greet, 0, unroll=7)
    for off in range(1, nx):
        for up in range(high):
            other = (lax.rem(hi + up, high) * low + lo, lax.rem(sub + off, nx))
            pl.semaphore_signal(barrier, inc=1, device_id=other, device_id_type=MESH)

    out_row = iota((LANES, LANES), 0)
    in_row = iota((LANES, LANES), 1)
    to_rows = jnp.where(in_row == lax.rem(out_row, ROWS) * OWNED + lax.div(out_row, ROWS), 1.0, 0.0)
    to_pairs = jnp.where(
        out_row == lax.rem(in_row, ROWS) * OWNED + lax.div(in_row, ROWS), 1.0, 0.0
    ).astype(BF16)
    load_c.wait()

    def fill(q):
        for g in range(PAIRS // 8):
            half = c_ref[:, g * 16 : (g + 1) * 16, q * WIDE : (q + 1) * WIDE]
            half = half.astype(BF16).reshape(LANES, WIDE)
            paired = jnp.dot(to_pairs, half, preferred_element_type=F32)
            deal[q, g * 8 : (g + 1) * 8] = paired.astype(BF16).reshape(8, ROWS, WIDE)

    fill(0)
    lane = iota((1, LANES), 1)
    code = jnp.zeros((1, LANES), jnp.int32)
    for i in range(NBLK):
        for j in range(CAND):
            here = lax.rem(lane, SLOTS)
            here = (lax.div(here, 2 * CAND) == i) & (lax.rem(here, CAND) == j)
            code = jnp.where(here, peer_ref[i, j] * ROWS + block_ref[i, j], code)
    code = code + OWNED * lax.rem(lax.div(lane, CAND), 2)
    req_ref[...] = jnp.where(lax.div(lane, SLOTS) == lax.rem(me, 4), code, 0).astype(F32)

    pl.semaphore_wait(barrier, n - 1 + (nx - 1) * high)

    def send(src_of, dst_of, sem):
        def body(off, carry):
            k = lax.rem(me + off, n)
            pltpu.make_async_remote_copy(
                src_ref=src_of(k),
                dst_ref=dst_of(me),
                send_sem=send_sem.at[sem],
                recv_sem=recv_sem.at[sem],
                device_id=(k, sub),
                device_id_type=MESH,
            ).start()
            return carry

        lax.fori_loop(1, n, body, 0, unroll=7)
        pltpu.make_async_copy(src_of(me), dst_of(me), recv_sem.at[sem]).start()

    REQ, GAP_LO, GAP_HI, W4, W6, S1, S1_REST = range(7)
    S3, S4, S6 = (7 + NQ * s for s in range(3))

    def mine(k):
        return pl.ds(k * rp, rp)

    rest = pl.ds(1, NQ - 1)
    send(lambda k: deal.at[0, mine(k)], lambda k: held.at[0, k], S1)
    send(lambda k: req_ref, lambda k: rq.at[k], REQ)
    for q in range(1, NQ):
        fill(q)
    send(lambda k: deal.at[rest, mine(k)], lambda k: held.at[rest, k], S1_REST)

    wait_bytes(rq, recv_sem.at[REQ])

    def build(d, carry):
        here = iota((SLOTS, LANES), 1) == lax.rem(d, 4) * SLOTS + iota((SLOTS, LANES), 0)
        code = jnp.sum(jnp.where(here, rq[d], 0.0), axis=1, keepdims=True)
        for t in range(keys // LANES):
            lane = (iota((SLOTS, LANES), 1) + t * LANES).astype(F32)
            onehot[d, :, t * LANES : (t + 1) * LANES] = jnp.where(code == lane, 1.0, 0.0).astype(BF16)
        return carry

    lax.fori_loop(0, n, build, 0)
    some = 8
    for q in range(NQ):
        if q == 0:
            wait_bytes(held.at[0], recv_sem.at[S1])
        if q == 1:
            wait_bytes(held.at[rest], recv_sem.at[S1_REST])

        def select(b, carry):
            here = pl.ds(b * some, some)
            table = onehot[here].reshape(some * SLOTS, keys)
            for r in range(rp):
                chosen = jnp.dot(
                    table, held[q, :, r].reshape(keys, WIDE), preferred_element_type=F32
                )
                pick[q, here, r] = chosen.astype(BF16).reshape(some, SLOTS, WIDE)
            return carry

        lax.fori_loop(0, n // some, select, 0)
        send(lambda k: pick.at[q, k], lambda k: got.at[q, mine(k)], S3 + q)

    load_x.wait()
    src = iota((NBLK * LANES, NBLK * LANES), 0)
    dst = lax.div(lax.rem(src, LANES), 32) * LANES + lax.div(lax.rem(src, 32), 8) * 32
    dst = dst + lax.div(src, LANES) * 8 + lax.rem(src, 8)
    pack[...] = jnp.where(iota((NBLK * LANES, NBLK * LANES), 1) == dst, 1.0, 0.0).astype(BF16)
    key = iota((keys, LANES), 0).astype(F32)
    for t in range(n // 4):
        code = rq[4 * t] + rq[4 * t + 1] + rq[4 * t + 2] + rq[4 * t + 3]
        onehot_t[:, t * LANES : (t + 1) * LANES] = jnp.where(key == code, 1.0, 0.0).astype(BF16)
    square = jnp.zeros((x_ref.shape[0], LANES), F32)
    for t in range(NQ * WIDE // LANES):
        square = square + jnp.square(x_ref[:, t * LANES : (t + 1) * LANES].astype(F32))
    xsq = lax.dot_general(
        jnp.ones((8, LANES), F32),
        square,
        (((1,), (1,)), ((), ())),
        preferred_element_type=F32,
        precision=lax.Precision.HIGHEST,
    )[:1]

    step = 32
    stats = []
    for q in range(NQ):
        cols = slice(q * WIDE, (q + 1) * WIDE)
        wait_bytes(got.at[q], recv_sem.at[S3 + q])
        for t in range(NBLK // 2):
            pts = slice(t * 2 * PBLK, (t + 1) * 2 * PBLK)

            def multiply(b, carry):
                here = pl.ds(b * step, step)
                rows = got[q, here, t * 16 : (t + 1) * 16].reshape(step * 16, WIDE)
                dots = lax.dot_general(
                    rows, x_ref[pts, cols], (((1,), (1,)), ((), ())), preferred_element_type=F32
                ).reshape(step, 2, 8, 2 * PBLK)
                wide = jnp.square(rows.astype(F32))
                sq = (wide[:, :LANES] + wide[:, LANES:]).reshape(step, 2, 8, LANES)
                after = []
                for i2 in range(2):
                    i = 2 * t + i2
                    dot = dots[:, i2, :, i2 * PBLK : (i2 + 1) * PBLK]
                    s = sq[:, i2]
                    if q > 0:
                        dot = dist[i, here] + dot
                        s = csq[i, here] + s
                    if q < NQ - 1:
                        dist[i, here] = dot
                        csq[i, here] = s
                    else:
                        x2 = xsq[:, i * PBLK : (i + 1) * PBLK]
                        d = (x2[None] + jnp.sum(s, axis=2, keepdims=True)) - 2.0 * dot
                        dist[i, here] = d
                        after.append(jnp.minimum(carry[2 * i2], jnp.min(d, axis=0)))
                        after.append(carry[2 * i2 + 1] + jnp.sum(d, axis=0))
                return tuple(after)

            start = ()
            if q == NQ - 1:
                start = (jnp.full((8, PBLK), jnp.inf, F32), jnp.zeros((8, PBLK), F32)) * 2
            found = lax.fori_loop(0, PAIRS // step, multiply, start)
            if q == NQ - 1:
                stats += [found[:2], found[2:]]
    least = [jnp.min(m, axis=0, keepdims=True) for m, _ in stats]
    gap = jnp.zeros((1, PBLK), F32)
    for i in range(NBLK):
        gap = gap + (jnp.sum(stats[i][1], axis=0, keepdims=True) / (CAND * CBLK) - least[i])

    gap_own[0] = jnp.broadcast_to(jnp.sum(gap, axis=1, keepdims=True), (1, LANES))

    def share(of, into, at, devices, sem):
        into[at] = gap_own[of]
        for device in devices:
            pltpu.make_async_remote_copy(
                src_ref=gap_own.at[of],
                dst_ref=into.at[at],
                send_sem=send_sem.at[sem],
                recv_sem=recv_sem.at[sem],
                device_id=device,
                device_id_type=MESH,
            ).start()
        if len(devices) > 0:
            wait_bytes(into.at[pl.ds(0, len(devices))], recv_sem.at[sem])
        return jnp.sum(into[...], axis=0)

    gap_own[1] = share(
        0, gap_lo, lo, [(hi * low + lax.rem(lo + o, low), sub) for o in range(1, low)], GAP_LO
    )
    across = high * nx
    place = hi * nx + sub
    others = [lax.rem(place + o, across) for o in range(1, across)]
    others = [(lax.div(o, nx) * low + lo, lax.rem(o, nx)) for o in others]
    every = share(1, gap_hi, place, others, GAP_HI)
    spread = every[:, :1] / total_points + 1e-6
    scale = 3.0 / spread

    for i in range(NBLK):

        def exponent(b, norm):
            here = pl.ds(b * step, step)
            e = jnp.exp((least[i][None] - dist[i, here]) * scale[None])
            dist[i, here] = e
            return norm + jnp.sum(e, axis=0)

        norm = lax.fori_loop(0, PAIRS // step, exponent, jnp.zeros((8, PBLK), F32))
        inverse = 1.0 / jnp.sum(norm, axis=0, keepdims=True)

        def normalise(b, carry):
            e = dist[i, pl.ds(b * step, step)]
            resp[i, pl.ds(b * step * 8, step * 8)] = (
                (e * inverse[None]).reshape(step * 8, PBLK).astype(BF16)
            )
            return carry

        lax.fori_loop(0, PAIRS // step, normalise, 0)

    tiles = max(1, rp // 4)

    for q in range(NQ):
        cols = slice(q * WIDE, (q + 1) * WIDE)

        def accumulate(b, carry):
            for t in range(NBLK // 2):
                two = [
                    jnp.dot(
                        resp[i],
                        x_ref[i * PBLK : (i + 1) * PBLK, cols],
                        preferred_element_type=F32,
                    ).reshape(PAIRS, 8, WIDE)
                    for i in (2 * t, 2 * t + 1)
                ]
                part[q, :, t * 16 : (t + 1) * 16] = jnp.concatenate(
                    two, axis=1
                ).astype(BF16)
            return carry

        accumulate(0, 0)
        send(lambda k: part.at[q, mine(k)], lambda k: back.at[q, k], S4 + q)
        if q == 0:
            tile = iota((8, LANES), 0)
            masses = []
            for i in range(NBLK):
                mass = lax.dot_general(
                    jnp.ones((8, PBLK), BF16),
                    resp[i],
                    (((1,), (1,)), ((), ())),
                    preferred_element_type=F32,
                )
                stacked = mass[:, :LANES]
                for t in range(1, CAND):
                    stacked = jnp.where(tile == t, mass[:, t * LANES : (t + 1) * LANES], stacked)
                masses.append(stacked)
            packed = jnp.concatenate(masses, axis=1).astype(BF16)
            packed = jnp.dot(packed, pack[...], preferred_element_type=F32)
            for t in range(CAND):
                for v in range(NBLK):
                    w_part[t * NBLK + v] = packed[t : t + 1, v * LANES : (v + 1) * LANES]
            send(
                lambda k: w_part.at[pl.ds(lax.div(k * rp, 4), tiles)], lambda k: w_back.at[k], W4
            )

    for q in range(NQ):
        wait_bytes(back.at[q], recv_sem.at[S4 + q])

        def combine(b, carry):
            table = onehot_t[pl.ds(b * some * ROWS, some * ROWS)]
            for r in range(rp):
                added = jnp.dot(
                    table, back[q, :, r].reshape(n * SLOTS, WIDE), preferred_element_type=F32
                )
                final[q, pl.ds(b * some, some), r] = added.astype(BF16).reshape(some, ROWS, WIDE)
            return carry

        lax.fori_loop(0, n // some, combine, 0)
        send(lambda k: final.at[q, k], lambda k: home.at[q, mine(k)], S6 + q)
        if q == 0:
            wait_bytes(w_back, recv_sem.at[W4])
            lane = iota((n, ROWS, LANES), 2)
            row = iota((n, ROWS, LANES), 1)
            weight = jnp.zeros((n, 1, LANES), F32)
            for r in range(rp):
                first = lax.rem(me * rp + r, 4) * SLOTS
                spot = iota((n, SLOTS, LANES), 2) == iota((n, SLOTS, LANES), 1) + first
                wide = jnp.where(spot, w_back[:, r // 4], 0.0)
                wide = wide.reshape(n * SLOTS, LANES).astype(BF16)
                added = jnp.dot(onehot_t[...], wide, preferred_element_type=F32)
                added = jnp.sum(added, axis=1, keepdims=True).reshape(n, ROWS, 1)
                weight = weight + jnp.sum(
                    jnp.where(lane == row + ROWS * r, added, 0.0), axis=1, keepdims=True
                )
            w_final[...] = weight
            send(lambda k: w_final.at[k], lambda k: w_home.at[k], W6)

    wait_bytes(w_home, recv_sem.at[W6])
    spot = iota((8, ROWS, LANES), 2) == iota((8, ROWS, LANES), 1) + ROWS * lax.rem(
        iota((8, ROWS, LANES), 0), rp
    )
    own = 8 // rp
    inverse = []
    for g in range(PAIRS // 8):
        wide = jnp.broadcast_to(w_home[g * own : (g + 1) * own][:, None], (own, rp, 1, LANES))
        wide = jnp.where(spot, wide.reshape(8, 1, LANES), 0.0).reshape(LANES, LANES)
        wide = jnp.dot(
            to_rows, wide, preferred_element_type=F32, precision=lax.Precision.HIGHEST
        )
        wide = 1.0 / (jnp.sum(wide, axis=1, keepdims=True) + 1.0)
        inverse.append(wide.reshape(OWNED, 16, 1))
    for q in range(NQ):
        cols = slice(q * WIDE, (q + 1) * WIDE)
        wait_bytes(home.at[q], recv_sem.at[S6 + q])
        for g in range(PAIRS // 8):
            sums = jnp.dot(
                to_rows.astype(BF16),
                home[q, g * 8 : (g + 1) * 8].reshape(LANES, WIDE),
                preferred_element_type=F32,
            ).reshape(OWNED, 16, WIDE)
            rows = slice(g * 16, (g + 1) * 16)
            out_ref[:, rows, cols] = (sums + 1.0 * c_ref[:, rows, cols]) * inverse[g]
        pltpu.make_async_copy(
            out_ref.at[:, :, cols], out_hbm.at[:, :, cols], out_sem.at[q]
        ).start()

    others = pl.ds(0, n - 1)
    wait_bytes(rq.at[others], send_sem.at[REQ])
    wait_bytes(gap_lo.at[pl.ds(0, low - 1)], send_sem.at[GAP_LO])
    wait_bytes(gap_hi.at[pl.ds(0, across - 1)], send_sem.at[GAP_HI])
    wait_bytes(w_back.at[others], send_sem.at[W4])
    wait_bytes(w_final.at[others], send_sem.at[W6])
    wait_bytes(held.at[0, others], send_sem.at[S1])
    wait_bytes(held.at[rest, others], send_sem.at[S1_REST])
    for q in range(NQ):
        wait_bytes(pick.at[q, others], send_sem.at[S3 + q])
        wait_bytes(back.at[q, others], send_sem.at[S4 + q])
        wait_bytes(final.at[q, others], send_sem.at[S6 + q])
    for q in range(NQ):
        cols = slice(q * WIDE, (q + 1) * WIDE)
        pltpu.make_async_copy(
            out_ref.at[:, :, cols], out_hbm.at[:, :, cols], out_sem.at[q]
        ).wait()


def on_device(n, nx, points, centroids, cand_peer, cand_block):
    rp = PAIRS // n
    pts, width = points.shape
    smem = pl.BlockSpec(memory_space=pltpu.SMEM)
    n_sem = 7 + 3 * NQ
    low = 16 if n >= 64 else 4
    hbm = pl.BlockSpec(memory_space=pl.ANY)
    refined = pl.pallas_call(
        functools.partial(kernel, n, nx, pts * n * nx),
        out_shape=jax.ShapeDtypeStruct((OWNED, CBLK, width), F32),
        in_specs=[hbm, hbm, smem, smem],
        out_specs=hbm,
        scratch_shapes=[
            pltpu.VMEM((1, LANES), F32),
            pltpu.VMEM((OWNED, CBLK, width), F32),
            pltpu.VMEM((pts, width), BF16),
            pltpu.VMEM((OWNED, CBLK, width), F32),
            pltpu.VMEM((n, 1, LANES), F32),
            pltpu.VMEM((n, SLOTS, n * ROWS), BF16),
            pltpu.VMEM((n * ROWS, n * SLOTS), BF16),
            pltpu.VMEM((NQ, PAIRS, ROWS, WIDE), BF16),
            pltpu.VMEM((NQ, n, rp, ROWS, WIDE), BF16),
            pltpu.VMEM((NQ, n, rp, SLOTS, WIDE), BF16),
            pltpu.VMEM((NQ, PAIRS, SLOTS, WIDE), BF16),
            pltpu.VMEM((NBLK, PAIRS, 8, LANES), F32),
            pltpu.VMEM((NBLK, PAIRS, 8, PBLK), F32),
            pltpu.VMEM((NBLK, PAIRS * 8, PBLK), BF16),
            pltpu.VMEM((NBLK * LANES, NBLK * LANES), BF16),
            pltpu.VMEM((NQ, PAIRS, SLOTS, WIDE), BF16),
            pltpu.VMEM((NQ, n, rp, SLOTS, WIDE), BF16),
            pltpu.VMEM((NQ, n, rp, ROWS, WIDE), BF16),
            pltpu.VMEM((NQ, PAIRS, ROWS, WIDE), BF16),
            pltpu.VMEM((PAIRS // 4, 1, LANES), F32),
            pltpu.VMEM((n, max(1, rp // 4), 1, LANES), F32),
            pltpu.VMEM((n, 1, LANES), F32),
            pltpu.VMEM((n, 1, LANES), F32),
            pltpu.VMEM((2, 1, LANES), F32),
            pltpu.VMEM((low, 1, LANES), F32),
            pltpu.VMEM((n // low * nx, 1, LANES), F32),
            pltpu.SemaphoreType.DMA((n_sem,)),
            pltpu.SemaphoreType.DMA((n_sem,)),
            pltpu.SemaphoreType.DMA((2,)),
            pltpu.SemaphoreType.DMA((NQ,)),
        ],
        compiler_params=pltpu.CompilerParams(
            collective_id=0, has_side_effects=True, vmem_limit_bytes=VMEM_LIMIT
        ),
    )(points, centroids.reshape(OWNED, CBLK, width), cand_peer, cand_block)
    return refined.reshape(OWNED * CBLK, width)


def solution(mesh):
    placed = P(("shard", "sub"), None)
    body = functools.partial(on_device, mesh.shape["shard"], mesh.shape["sub"])
    return jax.shard_map(
        body, mesh=mesh, in_specs=(placed,) * 4, out_specs=placed, check_vma=False
    )
```

```python
import functools

import jax
import jax.numpy as jnp
from jax import lax
from jax.experimental import pallas as pl
from jax.experimental.pallas import tpu as pltpu
from jax.sharding import PartitionSpec as P

PBLK = 256
CBLK = 128
CAND = 4
NBLK = 4
OWNED = 8
PAIRS = CBLK // 2
ROWS = 2 * OWNED
SLOTS = 2 * NBLK * CAND
NQ = 3
WIDE = 256
LANES = 128
VMEM_LIMIT = 56 * 1024 * 1024
MESH = pl.DeviceIdType.MESH
F32 = jnp.float32
BF16 = jnp.bfloat16


def wait_bytes(ref, sem):
    pltpu.make_async_copy(ref, ref, sem).wait()


def iota(shape, dim):
    return lax.broadcasted_iota(jnp.int32, shape, dim)


def kernel(
    n,
    nx,
    total_points,
    x_hbm,
    c_hbm,
    peer_ref,
    block_ref,
    out_hbm,
    req_ref,
    out_ref,
    x_ref,
    c_ref,
    rq,
    onehot,
    onehot_t,
    deal,
    held,
    pick,
    got,
    csq,
    dist,
    resp,
    pack,
    part,
    back,
    final,
    home,
    w_part,
    w_back,
    w_final,
    w_home,
    gap_own,
    gap_lo,
    gap_hi,
    send_sem,
    recv_sem,
    load_sem,
    out_sem,
):
    rp = PAIRS // n
    keys = n * ROWS
    low = gap_lo.shape[0]
    high = n // low
    me = lax.axis_index("shard")
    sub = lax.axis_index("sub")
    lo = lax.rem(me, low)
    hi = lax.div(me, low)

    load_c = pltpu.make_async_copy(c_hbm, c_ref, load_sem.at[0])
    load_x = pltpu.make_async_copy(x_hbm, x_ref, load_sem.at[1])
    load_c.start()
    load_x.start()

    barrier = pltpu.get_barrier_semaphore()

    def greet(off, carry):
        pl.semaphore_signal(
            barrier, inc=1, device_id=(lax.rem(me + off, n), sub), device_id_type=MESH
        )
        return carry

    lax.fori_loop(1, n, greet, 0, unroll=7)
    for off in range(1, nx):
        for up in range(high):
            other = (lax.rem(hi + up, high) * low + lo, lax.rem(sub + off, nx))
            pl.semaphore_signal(barrier, inc=1, device_id=other, device_id_type=MESH)

    out_row = iota((LANES, LANES), 0)
    in_row = iota((LANES, LANES), 1)
    to_rows = jnp.where(in_row == lax.rem(out_row, ROWS) * OWNED + lax.div(out_row, ROWS), 1.0, 0.0)
    to_pairs = jnp.where(
        out_row == lax.rem(in_row, ROWS) * OWNED + lax.div(in_row, ROWS), 1.0, 0.0
    ).astype(BF16)
    load_c.wait()

    def fill(q):
        for g in range(PAIRS // 8):
            half = c_ref[:, g * 16 : (g + 1) * 16, q * WIDE : (q + 1) * WIDE]
            half = half.astype(BF16).reshape(LANES, WIDE)
            paired = jnp.dot(to_pairs, half, preferred_element_type=F32)
            deal[q, g * 8 : (g + 1) * 8] = paired.astype(BF16).reshape(8, ROWS, WIDE)

    fill(0)
    lane = iota((1, LANES), 1)
    code = jnp.zeros((1, LANES), jnp.int32)
    for i in range(NBLK):
        for j in range(CAND):
            here = lax.rem(lane, SLOTS)
            here = (lax.div(here, 2 * CAND) == i) & (lax.rem(here, CAND) == j)
            code = jnp.where(here, peer_ref[i, j] * ROWS + block_ref[i, j], code)
    code = code + OWNED * lax.rem(lax.div(lane, CAND), 2)
    req_ref[...] = jnp.where(lax.div(lane, SLOTS) == lax.rem(me, 4), code, 0).astype(F32)

    pl.semaphore_wait(barrier, n - 1 + (nx - 1) * high)

    def send(src_of, dst_of, sem):
        def body(off, carry):
            k = lax.rem(me + off, n)
            pltpu.make_async_remote_copy(
                src_ref=src_of(k),
                dst_ref=dst_of(me),
                send_sem=send_sem.at[sem],
                recv_sem=recv_sem.at[sem],
                device_id=(k, sub),
                device_id_type=MESH,
            ).start()
            return carry

        lax.fori_loop(1, n, body, 0, unroll=7)
        pltpu.make_async_copy(src_of(me), dst_of(me), recv_sem.at[sem]).start()

    REQ, GAP_LO, GAP_HI, W4, W6, S1, S1_REST = range(7)
    S3, S4, S6 = (7 + NQ * s for s in range(3))

    def mine(k):
        return pl.ds(k * rp, rp)

    rest = pl.ds(1, NQ - 1)
    send(lambda k: deal.at[0, mine(k)], lambda k: held.at[0, k], S1)
    send(lambda k: req_ref, lambda k: rq.at[k], REQ)
    for q in range(1, NQ):
        fill(q)
    send(lambda k: deal.at[rest, mine(k)], lambda k: held.at[rest, k], S1_REST)

    wait_bytes(rq, recv_sem.at[REQ])

    def build(d, carry):
        here = iota((SLOTS, LANES), 1) == lax.rem(d, 4) * SLOTS + iota((SLOTS, LANES), 0)
        code = jnp.sum(jnp.where(here, rq[d], 0.0), axis=1, keepdims=True)
        for t in range(keys // LANES):
            lane = (iota((SLOTS, LANES), 1) + t * LANES).astype(F32)
            onehot[d, :, t * LANES : (t + 1) * LANES] = jnp.where(code == lane, 1.0, 0.0).astype(BF16)
        return carry

    lax.fori_loop(0, n, build, 0)
    some = min(16, n)
    many = min(32, n)
    for q in range(NQ):
        if q == 0:
            wait_bytes(held.at[0], recv_sem.at[S1])
        if q == 1:
            wait_bytes(held.at[rest], recv_sem.at[S1_REST])

        def select(b, carry):
            here = pl.ds(b * some, some)
            table = onehot[here].reshape(some * SLOTS, keys)
            for r in range(rp):
                chosen = jnp.dot(
                    table, held[q, :, r].reshape(keys, WIDE), preferred_element_type=F32
                )
                pick[q, here, r] = chosen.astype(BF16).reshape(some, SLOTS, WIDE)
            return carry

        lax.fori_loop(0, n // some, select, 0)
        send(lambda k: pick.at[q, k], lambda k: got.at[q, mine(k)], S3 + q)

    load_x.wait()
    src = iota((NBLK * LANES, NBLK * LANES), 0)
    dst = lax.div(lax.rem(src, LANES), 32) * LANES + lax.div(lax.rem(src, 32), 8) * 32
    dst = dst + lax.div(src, LANES) * 8 + lax.rem(src, 8)
    pack[...] = jnp.where(iota((NBLK * LANES, NBLK * LANES), 1) == dst, 1.0, 0.0).astype(BF16)
    key = iota((keys, LANES), 0).astype(F32)
    for t in range(n // 4):
        code = rq[4 * t] + rq[4 * t + 1] + rq[4 * t + 2] + rq[4 * t + 3]
        onehot_t[:, t * LANES : (t + 1) * LANES] = jnp.where(key == code, 1.0, 0.0).astype(BF16)
    square = jnp.zeros((x_ref.shape[0], LANES), F32)
    for t in range(NQ * WIDE // LANES):
        square = square + jnp.square(x_ref[:, t * LANES : (t + 1) * LANES].astype(F32))
    xsq = lax.dot_general(
        jnp.ones((8, LANES), F32),
        square,
        (((1,), (1,)), ((), ())),
        preferred_element_type=F32,
        precision=lax.Precision.HIGHEST,
    )[:1]

    step = 64
    stats = []
    for q in range(NQ):
        cols = slice(q * WIDE, (q + 1) * WIDE)
        wait_bytes(got.at[q], recv_sem.at[S3 + q])
        for t in range(NBLK // 2):
            pts = slice(t * 2 * PBLK, (t + 1) * 2 * PBLK)

            def multiply(b, carry):
                here = pl.ds(b * step, step)
                rows = got[q, here, t * 16 : (t + 1) * 16].reshape(step * 16, WIDE)
                dots = lax.dot_general(
                    rows, x_ref[pts, cols], (((1,), (1,)), ((), ())), preferred_element_type=F32
                ).reshape(step, 2, 8, 2 * PBLK)
                wide = jnp.square(rows.astype(F32))
                sq = (wide[:, :LANES] + wide[:, LANES:]).reshape(step, 2, 8, LANES)
                after = []
                for i2 in range(2):
                    i = 2 * t + i2
                    dot = dots[:, i2, :, i2 * PBLK : (i2 + 1) * PBLK]
                    s = sq[:, i2]
                    if q > 0:
                        dot = dist[i, here] + dot
                        s = csq[i, here] + s
                    if q < NQ - 1:
                        dist[i, here] = dot
                        csq[i, here] = s
                    else:
                        x2 = xsq[:, i * PBLK : (i + 1) * PBLK]
                        d = (x2[None] + jnp.sum(s, axis=2, keepdims=True)) - 2.0 * dot
                        dist[i, here] = d
                        after.append(jnp.minimum(carry[2 * i2], jnp.min(d, axis=0)))
                        after.append(carry[2 * i2 + 1] + jnp.sum(d, axis=0))
                return tuple(after)

            start = ()
            if q == NQ - 1:
                start = (jnp.full((8, PBLK), jnp.inf, F32), jnp.zeros((8, PBLK), F32)) * 2
            found = lax.fori_loop(0, PAIRS // step, multiply, start)
            if q == NQ - 1:
                stats += [found[:2], found[2:]]
    least = [jnp.min(m, axis=0, keepdims=True) for m, _ in stats]
    gap = jnp.zeros((1, PBLK), F32)
    for i in range(NBLK):
        gap = gap + (jnp.sum(stats[i][1], axis=0, keepdims=True) / (CAND * CBLK) - least[i])

    gap_own[0] = jnp.broadcast_to(jnp.sum(gap, axis=1, keepdims=True), (1, LANES))

    def share(of, into, at, devices, sem):
        into[at] = gap_own[of]
        for device in devices:
            pltpu.make_async_remote_copy(
                src_ref=gap_own.at[of],
                dst_ref=into.at[at],
                send_sem=send_sem.at[sem],
                recv_sem=recv_sem.at[sem],
                device_id=device,
                device_id_type=MESH,
            ).start()
        if len(devices) > 0:
            wait_bytes(into.at[pl.ds(0, len(devices))], recv_sem.at[sem])
        return jnp.sum(into[...], axis=0)

    gap_own[1] = share(
        0, gap_lo, lo, [(hi * low + lax.rem(lo + o, low), sub) for o in range(1, low)], GAP_LO
    )
    across = high * nx
    place = hi * nx + sub
    others = [lax.rem(place + o, across) for o in range(1, across)]
    others = [(lax.div(o, nx) * low + lo, lax.rem(o, nx)) for o in others]
    every = share(1, gap_hi, place, others, GAP_HI)
    spread = every[:, :1] / total_points + 1e-6
    scale = 3.0 / spread

    for i in range(NBLK):

        def exponent(b, norm):
            here = pl.ds(b * step, step)
            e = jnp.exp((least[i][None] - dist[i, here]) * scale[None])
            dist[i, here] = e
            return norm + jnp.sum(e, axis=0)

        norm = lax.fori_loop(0, PAIRS // step, exponent, jnp.zeros((8, PBLK), F32))
        inverse = 1.0 / jnp.sum(norm, axis=0, keepdims=True)

        def normalise(b, carry):
            e = dist[i, pl.ds(b * step, step)]
            resp[i, pl.ds(b * step * 8, step * 8)] = (
                (e * inverse[None]).reshape(step * 8, PBLK).astype(BF16)
            )
            return carry

        lax.fori_loop(0, PAIRS // step, normalise, 0)

    tiles = max(1, rp // 4)

    for q in range(NQ):
        cols = slice(q * WIDE, (q + 1) * WIDE)

        def accumulate(b, carry):
            for t in range(NBLK // 2):
                two = [
                    jnp.dot(
                        resp[i],
                        x_ref[i * PBLK : (i + 1) * PBLK, cols],
                        preferred_element_type=F32,
                    ).reshape(PAIRS, 8, WIDE)
                    for i in (2 * t, 2 * t + 1)
                ]
                part[q, :, t * 16 : (t + 1) * 16] = jnp.concatenate(
                    two, axis=1
                ).astype(BF16)
            return carry

        accumulate(0, 0)
        send(lambda k: part.at[q, mine(k)], lambda k: back.at[q, k], S4 + q)
        if q == 0:
            tile = iota((8, LANES), 0)
            masses = []
            for i in range(NBLK):
                mass = lax.dot_general(
                    jnp.ones((8, PBLK), BF16),
                    resp[i],
                    (((1,), (1,)), ((), ())),
                    preferred_element_type=F32,
                )
                stacked = mass[:, :LANES]
                for t in range(1, CAND):
                    stacked = jnp.where(tile == t, mass[:, t * LANES : (t + 1) * LANES], stacked)
                masses.append(stacked)
            packed = jnp.concatenate(masses, axis=1).astype(BF16)
            packed = jnp.dot(packed, pack[...], preferred_element_type=F32)
            for t in range(CAND):
                for v in range(NBLK):
                    w_part[t * NBLK + v] = packed[t : t + 1, v * LANES : (v + 1) * LANES]
            send(
                lambda k: w_part.at[pl.ds(lax.div(k * rp, 4), tiles)], lambda k: w_back.at[k], W4
            )

    for q in range(NQ):
        wait_bytes(back.at[q], recv_sem.at[S4 + q])

        def combine(b, carry):
            table = onehot_t[pl.ds(b * many * ROWS, many * ROWS)]
            for r in range(rp):
                added = jnp.dot(
                    table, back[q, :, r].reshape(n * SLOTS, WIDE), preferred_element_type=F32
                )
                final[q, pl.ds(b * many, many), r] = added.astype(BF16).reshape(many, ROWS, WIDE)
            return carry

        lax.fori_loop(0, n // many, combine, 0)
        send(lambda k: final.at[q, k], lambda k: home.at[q, mine(k)], S6 + q)
        if q == 0:
            wait_bytes(w_back, recv_sem.at[W4])
            lane = iota((n, ROWS, LANES), 2)
            row = iota((n, ROWS, LANES), 1)
            weight = jnp.zeros((n, 1, LANES), F32)
            for r in range(rp):
                first = lax.rem(me * rp + r, 4) * SLOTS
                spot = iota((n, SLOTS, LANES), 2) == iota((n, SLOTS, LANES), 1) + first
                wide = jnp.where(spot, w_back[:, r // 4], 0.0)
                wide = wide.reshape(n * SLOTS, LANES).astype(BF16)
                added = jnp.dot(onehot_t[...], wide, preferred_element_type=F32)
                added = jnp.sum(added, axis=1, keepdims=True).reshape(n, ROWS, 1)
                weight = weight + jnp.sum(
                    jnp.where(lane == row + ROWS * r, added, 0.0), axis=1, keepdims=True
                )
            w_final[...] = weight
            send(lambda k: w_final.at[k], lambda k: w_home.at[k], W6)

    wait_bytes(w_home, recv_sem.at[W6])
    spot = iota((8, ROWS, LANES), 2) == iota((8, ROWS, LANES), 1) + ROWS * lax.rem(
        iota((8, ROWS, LANES), 0), rp
    )
    own = 8 // rp
    inverse = []
    for g in range(PAIRS // 8):
        wide = jnp.broadcast_to(w_home[g * own : (g + 1) * own][:, None], (own, rp, 1, LANES))
        wide = jnp.where(spot, wide.reshape(8, 1, LANES), 0.0).reshape(LANES, LANES)
        wide = jnp.dot(
            to_rows, wide, preferred_element_type=F32, precision=lax.Precision.HIGHEST
        )
        wide = 1.0 / (jnp.sum(wide, axis=1, keepdims=True) + 1.0)
        inverse.append(wide.reshape(OWNED, 16, 1))
    for q in range(NQ):
        cols = slice(q * WIDE, (q + 1) * WIDE)
        wait_bytes(home.at[q], recv_sem.at[S6 + q])
        for g in range(PAIRS // 8):
            sums = jnp.dot(
                to_rows.astype(BF16),
                home[q, g * 8 : (g + 1) * 8].reshape(LANES, WIDE),
                preferred_element_type=F32,
            ).reshape(OWNED, 16, WIDE)
            rows = slice(g * 16, (g + 1) * 16)
            out_ref[:, rows, cols] = (sums + 1.0 * c_ref[:, rows, cols]) * inverse[g]
        pltpu.make_async_copy(
            out_ref.at[:, :, cols], out_hbm.at[:, :, cols], out_sem.at[q]
        ).start()

    others = pl.ds(0, n - 1)
    wait_bytes(rq.at[others], send_sem.at[REQ])
    wait_bytes(gap_lo.at[pl.ds(0, low - 1)], send_sem.at[GAP_LO])
    wait_bytes(gap_hi.at[pl.ds(0, across - 1)], send_sem.at[GAP_HI])
    wait_bytes(w_back.at[others], send_sem.at[W4])
    wait_bytes(w_final.at[others], send_sem.at[W6])
    wait_bytes(held.at[0, others], send_sem.at[S1])
    wait_bytes(held.at[rest, others], send_sem.at[S1_REST])
    for q in range(NQ):
        wait_bytes(pick.at[q, others], send_sem.at[S3 + q])
        wait_bytes(back.at[q, others], send_sem.at[S4 + q])
        wait_bytes(final.at[q, others], send_sem.at[S6 + q])
    for q in range(NQ):
        cols = slice(q * WIDE, (q + 1) * WIDE)
        pltpu.make_async_copy(
            out_ref.at[:, :, cols], out_hbm.at[:, :, cols], out_sem.at[q]
        ).wait()


def on_device(n, nx, points, centroids, cand_peer, cand_block):
    rp = PAIRS // n
    pts, width = points.shape
    smem = pl.BlockSpec(memory_space=pltpu.SMEM)
    n_sem = 7 + 3 * NQ
    low = 16 if n >= 64 else 4
    hbm = pl.BlockSpec(memory_space=pl.ANY)
    refined = pl.pallas_call(
        functools.partial(kernel, n, nx, pts * n * nx),
        out_shape=jax.ShapeDtypeStruct((OWNED, CBLK, width), F32),
        in_specs=[hbm, hbm, smem, smem],
        out_specs=hbm,
        scratch_shapes=[
            pltpu.VMEM((1, LANES), F32),
            pltpu.VMEM((OWNED, CBLK, width), F32),
            pltpu.VMEM((pts, width), BF16),
            pltpu.VMEM((OWNED, CBLK, width), F32),
            pltpu.VMEM((n, 1, LANES), F32),
            pltpu.VMEM((n, SLOTS, n * ROWS), BF16),
            pltpu.VMEM((n * ROWS, n * SLOTS), BF16),
            pltpu.VMEM((NQ, PAIRS, ROWS, WIDE), BF16),
            pltpu.VMEM((NQ, n, rp, ROWS, WIDE), BF16),
            pltpu.VMEM((NQ, n, rp, SLOTS, WIDE), BF16),
            pltpu.VMEM((NQ, PAIRS, SLOTS, WIDE), BF16),
            pltpu.VMEM((NBLK, PAIRS, 8, LANES), F32),
            pltpu.VMEM((NBLK, PAIRS, 8, PBLK), F32),
            pltpu.VMEM((NBLK, PAIRS * 8, PBLK), BF16),
            pltpu.VMEM((NBLK * LANES, NBLK * LANES), BF16),
            pltpu.VMEM((NQ, PAIRS, SLOTS, WIDE), BF16),
            pltpu.VMEM((NQ, n, rp, SLOTS, WIDE), BF16),
            pltpu.VMEM((NQ, n, rp, ROWS, WIDE), BF16),
            pltpu.VMEM((NQ, PAIRS, ROWS, WIDE), BF16),
            pltpu.VMEM((PAIRS // 4, 1, LANES), F32),
            pltpu.VMEM((n, max(1, rp // 4), 1, LANES), F32),
            pltpu.VMEM((n, 1, LANES), F32),
            pltpu.VMEM((n, 1, LANES), F32),
            pltpu.VMEM((2, 1, LANES), F32),
            pltpu.VMEM((low, 1, LANES), F32),
            pltpu.VMEM((n // low * nx, 1, LANES), F32),
            pltpu.SemaphoreType.DMA((n_sem,)),
            pltpu.SemaphoreType.DMA((n_sem,)),
            pltpu.SemaphoreType.DMA((2,)),
            pltpu.SemaphoreType.DMA((NQ,)),
        ],
        compiler_params=pltpu.CompilerParams(
            collective_id=0, has_side_effects=True, vmem_limit_bytes=VMEM_LIMIT
        ),
    )(points, centroids.reshape(OWNED, CBLK, width), cand_peer, cand_block)
    return refined.reshape(OWNED * CBLK, width)


def solution(mesh):
    placed = P(("shard", "sub"), None)
    body = functools.partial(on_device, mesh.shape["shard"], mesh.shape["sub"])
    return jax.shard_map(
        body, mesh=mesh, in_specs=(placed,) * 4, out_specs=placed, check_vma=False
    )
```

```python
import functools

import jax
import jax.numpy as jnp
from jax import lax
from jax.experimental import pallas as pl
from jax.experimental.pallas import tpu as pltpu
from jax.sharding import PartitionSpec as P

PBLK = 256
CBLK = 128
CAND = 4
NBLK = 4
OWNED = 8
PAIRS = CBLK // 2
ROWS = 2 * OWNED
SLOTS = 2 * NBLK * CAND
NQ = 3
WIDE = 256
LANES = 128
VMEM_LIMIT = 56 * 1024 * 1024
MESH = pl.DeviceIdType.MESH
F32 = jnp.float32
BF16 = jnp.bfloat16


def wait_bytes(ref, sem):
    pltpu.make_async_copy(ref, ref, sem).wait()


def iota(shape, dim):
    return lax.broadcasted_iota(jnp.int32, shape, dim)


def kernel(
    n,
    nx,
    total_points,
    x_hbm,
    c_hbm,
    peer_ref,
    block_ref,
    out_hbm,
    req_ref,
    out_ref,
    x_ref,
    c_ref,
    rq,
    onehot,
    onehot_t,
    deal,
    held,
    pick,
    got,
    csq,
    dist,
    resp,
    pack,
    part,
    back,
    final,
    home,
    w_part,
    w_back,
    w_final,
    w_home,
    gap_own,
    gap_lo,
    gap_hi,
    send_sem,
    recv_sem,
    load_sem,
    out_sem,
):
    rp = PAIRS // n
    keys = n * ROWS
    low = gap_lo.shape[0]
    high = n // low
    me = lax.axis_index("shard")
    sub = lax.axis_index("sub")
    lo = lax.rem(me, low)
    hi = lax.div(me, low)

    load_c = pltpu.make_async_copy(c_hbm, c_ref, load_sem.at[0])
    load_x = pltpu.make_async_copy(x_hbm, x_ref, load_sem.at[1])
    load_c.start()
    load_x.start()

    barrier = pltpu.get_barrier_semaphore()

    def greet(off, carry):
        pl.semaphore_signal(
            barrier, inc=1, device_id=(lax.rem(me + off, n), sub), device_id_type=MESH
        )
        return carry

    lax.fori_loop(1, n, greet, 0, unroll=7)
    for off in range(1, nx):
        for up in range(high):
            other = (lax.rem(hi + up, high) * low + lo, lax.rem(sub + off, nx))
            pl.semaphore_signal(barrier, inc=1, device_id=other, device_id_type=MESH)

    out_row = iota((LANES, LANES), 0)
    in_row = iota((LANES, LANES), 1)
    to_rows = jnp.where(in_row == lax.rem(out_row, ROWS) * OWNED + lax.div(out_row, ROWS), 1.0, 0.0)
    to_pairs = jnp.where(
        out_row == lax.rem(in_row, ROWS) * OWNED + lax.div(in_row, ROWS), 1.0, 0.0
    ).astype(BF16)
    load_c.wait()

    def fill(q):
        for g in range(PAIRS // 8):
            half = c_ref[:, g * 16 : (g + 1) * 16, q * WIDE : (q + 1) * WIDE]
            half = half.astype(BF16).reshape(LANES, WIDE)
            paired = jnp.dot(to_pairs, half, preferred_element_type=F32)
            deal[q, g * 8 : (g + 1) * 8] = paired.astype(BF16).reshape(8, ROWS, WIDE)

    fill(0)
    lane = iota((1, LANES), 1)
    code = jnp.zeros((1, LANES), jnp.int32)
    for i in range(NBLK):
        for j in range(CAND):
            here = lax.rem(lane, SLOTS)
            here = (lax.div(here, 2 * CAND) == i) & (lax.rem(here, CAND) == j)
            code = jnp.where(here, peer_ref[i, j] * ROWS + block_ref[i, j], code)
    code = code + OWNED * lax.rem(lax.div(lane, CAND), 2)
    req_ref[...] = jnp.where(lax.div(lane, SLOTS) == lax.rem(me, 4), code, 0).astype(F32)

    pl.semaphore_wait(barrier, n - 1 + (nx - 1) * high)

    def send(src_of, dst_of, sem):
        def body(off, carry):
            k = lax.rem(me + off, n)
            pltpu.make_async_remote_copy(
                src_ref=src_of(k),
                dst_ref=dst_of(me),
                send_sem=send_sem.at[sem],
                recv_sem=recv_sem.at[sem],
                device_id=(k, sub),
                device_id_type=MESH,
            ).start()
            return carry

        lax.fori_loop(1, n, body, 0, unroll=7)
        pltpu.make_async_copy(src_of(me), dst_of(me), recv_sem.at[sem]).start()

    REQ, GAP_LO, GAP_HI, W4, W6, S1, S1_REST = range(7)
    S3, S4, S6 = (7 + NQ * s for s in range(3))

    def mine(k):
        return pl.ds(k * rp, rp)

    rest = pl.ds(1, NQ - 1)
    send(lambda k: deal.at[0, mine(k)], lambda k: held.at[0, k], S1)
    send(lambda k: req_ref, lambda k: rq.at[k], REQ)
    for q in range(1, NQ):
        fill(q)
    send(lambda k: deal.at[rest, mine(k)], lambda k: held.at[rest, k], S1_REST)

    wait_bytes(rq, recv_sem.at[REQ])

    def build(d, carry):
        here = iota((SLOTS, LANES), 1) == lax.rem(d, 4) * SLOTS + iota((SLOTS, LANES), 0)
        code = jnp.sum(jnp.where(here, rq[d], 0.0), axis=1, keepdims=True)
        for t in range(keys // LANES):
            lane = (iota((SLOTS, LANES), 1) + t * LANES).astype(F32)
            onehot[d, :, t * LANES : (t + 1) * LANES] = jnp.where(code == lane, 1.0, 0.0).astype(BF16)
        return carry

    lax.fori_loop(0, n, build, 0)
    some = min(16, n)
    many = min(32, n)
    for q in range(NQ):
        if q == 0:
            wait_bytes(held.at[0], recv_sem.at[S1])
        if q == 1:
            wait_bytes(held.at[rest], recv_sem.at[S1_REST])

        def select(b, carry):
            here = pl.ds(b * some, some)
            table = onehot[here].reshape(some * SLOTS, keys)
            for r in range(rp):
                chosen = jnp.dot(
                    table, held[q, :, r].reshape(keys, WIDE), preferred_element_type=F32
                )
                pick[q, here, r] = chosen.astype(BF16).reshape(some, SLOTS, WIDE)
            return carry

        lax.fori_loop(0, n // some, select, 0)
        send(lambda k: pick.at[q, k], lambda k: got.at[q, mine(k)], S3 + q)

    load_x.wait()
    src = iota((NBLK * LANES, NBLK * LANES), 0)
    dst = lax.div(lax.rem(src, LANES), 32) * LANES + lax.div(lax.rem(src, 32), 8) * 32
    dst = dst + lax.div(src, LANES) * 8 + lax.rem(src, 8)
    pack[...] = jnp.where(iota((NBLK * LANES, NBLK * LANES), 1) == dst, 1.0, 0.0).astype(BF16)
    key = iota((keys, LANES), 0).astype(F32)
    for t in range(n // 4):
        code = rq[4 * t] + rq[4 * t + 1] + rq[4 * t + 2] + rq[4 * t + 3]
        onehot_t[:, t * LANES : (t + 1) * LANES] = jnp.where(key == code, 1.0, 0.0).astype(BF16)
    square = jnp.zeros((x_ref.shape[0], LANES), F32)
    for t in range(NQ * WIDE // LANES):
        square = square + jnp.square(x_ref[:, t * LANES : (t + 1) * LANES].astype(F32))
    xsq = lax.dot_general(
        jnp.ones((8, LANES), F32),
        square,
        (((1,), (1,)), ((), ())),
        preferred_element_type=F32,
        precision=lax.Precision.HIGHEST,
    )[:1]

    step = 64
    stats = []
    for q in range(NQ):
        cols = slice(q * WIDE, (q + 1) * WIDE)
        wait_bytes(got.at[q], recv_sem.at[S3 + q])
        for t in range(NBLK // 2):
            pts = slice(t * 2 * PBLK, (t + 1) * 2 * PBLK)

            def multiply(b, carry):
                here = pl.ds(b * step, step)
                rows = got[q, here, t * 16 : (t + 1) * 16].reshape(step * 16, WIDE)
                dots = lax.dot_general(
                    rows, x_ref[pts, cols], (((1,), (1,)), ((), ())), preferred_element_type=F32
                ).reshape(step, 2, 8, 2 * PBLK)
                wide = jnp.square(rows.astype(F32))
                sq = (wide[:, :LANES] + wide[:, LANES:]).reshape(step, 2, 8, LANES)
                after = []
                for i2 in range(2):
                    i = 2 * t + i2
                    dot = dots[:, i2, :, i2 * PBLK : (i2 + 1) * PBLK]
                    s = sq[:, i2]
                    if q > 0:
                        dot = dist[i, here] + dot
                        s = csq[i, here] + s
                    if q < NQ - 1:
                        dist[i, here] = dot
                        csq[i, here] = s
                    else:
                        x2 = xsq[:, i * PBLK : (i + 1) * PBLK]
                        d = (x2[None] + jnp.sum(s, axis=2, keepdims=True)) - 2.0 * dot
                        dist[i, here] = d
                        after.append(jnp.minimum(carry[2 * i2], jnp.min(d, axis=0)))
                        after.append(carry[2 * i2 + 1] + jnp.sum(d, axis=0))
                return tuple(after)

            start = ()
            if q == NQ - 1:
                start = (jnp.full((8, PBLK), jnp.inf, F32), jnp.zeros((8, PBLK), F32)) * 2
            found = lax.fori_loop(0, PAIRS // step, multiply, start)
            if q == NQ - 1:
                stats += [found[:2], found[2:]]
    least = [jnp.min(m, axis=0, keepdims=True) for m, _ in stats]
    gap = jnp.zeros((1, PBLK), F32)
    for i in range(NBLK):
        gap = gap + (jnp.sum(stats[i][1], axis=0, keepdims=True) / (CAND * CBLK) - least[i])

    gap_own[0] = jnp.broadcast_to(jnp.sum(gap, axis=1, keepdims=True), (1, LANES))

    def share(of, into, at, devices, sem):
        into[at] = gap_own[of]
        for device in devices:
            pltpu.make_async_remote_copy(
                src_ref=gap_own.at[of],
                dst_ref=into.at[at],
                send_sem=send_sem.at[sem],
                recv_sem=recv_sem.at[sem],
                device_id=device,
                device_id_type=MESH,
            ).start()
        if len(devices) > 0:
            wait_bytes(into.at[pl.ds(0, len(devices))], recv_sem.at[sem])
        return jnp.sum(into[...], axis=0)

    gap_own[1] = share(
        0, gap_lo, lo, [(hi * low + lax.rem(lo + o, low), sub) for o in range(1, low)], GAP_LO
    )
    across = high * nx
    place = hi * nx + sub
    others = [lax.rem(place + o, across) for o in range(1, across)]
    others = [(lax.div(o, nx) * low + lo, lax.rem(o, nx)) for o in others]
    every = share(1, gap_hi, place, others, GAP_HI)
    spread = every[:, :1] / total_points + 1e-6
    scale = 3.0 / spread

    for i in range(NBLK):

        def exponent(b, norm):
            here = pl.ds(b * step, step)
            e = jnp.exp((least[i][None] - dist[i, here]) * scale[None])
            dist[i, here] = e
            return norm + jnp.sum(e, axis=0)

        norm = lax.fori_loop(0, PAIRS // step, exponent, jnp.zeros((8, PBLK), F32))
        inverse = 1.0 / jnp.sum(norm, axis=0, keepdims=True)

        def normalise(b, carry):
            e = dist[i, pl.ds(b * step, step)]
            resp[i, pl.ds(b * step * 8, step * 8)] = (
                (e * inverse[None]).reshape(step * 8, PBLK).astype(BF16)
            )
            return carry

        lax.fori_loop(0, PAIRS // step, normalise, 0)

    tiles = max(1, rp // 4)

    for q in range(NQ):
        cols = slice(q * WIDE, (q + 1) * WIDE)

        def accumulate(b, carry):
            for t in range(NBLK // 2):
                two = [
                    jnp.dot(
                        resp[i],
                        x_ref[i * PBLK : (i + 1) * PBLK, cols],
                        preferred_element_type=F32,
                    ).reshape(PAIRS, 8, WIDE)
                    for i in (2 * t, 2 * t + 1)
                ]
                part[q, :, t * 16 : (t + 1) * 16] = jnp.concatenate(
                    two, axis=1
                ).astype(BF16)
            return carry

        accumulate(0, 0)
        send(lambda k: part.at[q, mine(k)], lambda k: back.at[q, k], S4 + q)
        if q == 0:
            tile = iota((8, LANES), 0)
            masses = []
            for i in range(NBLK):
                mass = lax.dot_general(
                    jnp.ones((8, PBLK), BF16),
                    resp[i],
                    (((1,), (1,)), ((), ())),
                    preferred_element_type=F32,
                )
                stacked = mass[:, :LANES]
                for t in range(1, CAND):
                    stacked = jnp.where(tile == t, mass[:, t * LANES : (t + 1) * LANES], stacked)
                masses.append(stacked)
            packed = jnp.concatenate(masses, axis=1).astype(BF16)
            packed = jnp.dot(packed, pack[...], preferred_element_type=F32)
            for t in range(CAND):
                for v in range(NBLK):
                    w_part[t * NBLK + v] = packed[t : t + 1, v * LANES : (v + 1) * LANES]
            send(
                lambda k: w_part.at[pl.ds(lax.div(k * rp, 4), tiles)], lambda k: w_back.at[k], W4
            )

    for q in range(NQ):
        wait_bytes(back.at[q], recv_sem.at[S4 + q])

        def combine(b, carry):
            table = onehot_t[pl.ds(b * many * ROWS, many * ROWS)]
            for r in range(rp):
                added = jnp.dot(
                    table, back[q, :, r].reshape(n * SLOTS, WIDE), preferred_element_type=F32
                )
                final[q, pl.ds(b * many, many), r] = added.astype(BF16).reshape(many, ROWS, WIDE)
            return carry

        lax.fori_loop(0, n // many, combine, 0)
        send(lambda k: final.at[q, k], lambda k: home.at[q, mine(k)], S6 + q)
        if q == 0:
            wait_bytes(w_back, recv_sem.at[W4])
            lane = iota((n, ROWS, LANES), 2)
            row = iota((n, ROWS, LANES), 1)
            weight = jnp.zeros((n, 1, LANES), F32)
            for r in range(rp):
                first = lax.rem(me * rp + r, 4) * SLOTS
                spot = iota((n, SLOTS, LANES), 2) == iota((n, SLOTS, LANES), 1) + first
                wide = jnp.where(spot, w_back[:, r // 4], 0.0)
                wide = wide.reshape(n * SLOTS, LANES).astype(BF16)
                added = jnp.dot(onehot_t[...], wide, preferred_element_type=F32)
                added = jnp.sum(added, axis=1, keepdims=True).reshape(n, ROWS, 1)
                weight = weight + jnp.sum(
                    jnp.where(lane == row + ROWS * r, added, 0.0), axis=1, keepdims=True
                )
            w_final[...] = weight
            send(lambda k: w_final.at[k], lambda k: w_home.at[k], W6)

    wait_bytes(w_home, recv_sem.at[W6])
    spot = iota((8, ROWS, LANES), 2) == iota((8, ROWS, LANES), 1) + ROWS * lax.rem(
        iota((8, ROWS, LANES), 0), rp
    )
    own = 8 // rp
    inverse = []
    for g in range(PAIRS // 8):
        wide = jnp.broadcast_to(w_home[g * own : (g + 1) * own][:, None], (own, rp, 1, LANES))
        wide = jnp.where(spot, wide.reshape(8, 1, LANES), 0.0).reshape(LANES, LANES)
        wide = jnp.dot(
            to_rows, wide, preferred_element_type=F32, precision=lax.Precision.HIGHEST
        )
        wide = 1.0 / (jnp.sum(wide, axis=1, keepdims=True) + 1.0)
        inverse.append(wide.reshape(OWNED, 16, 1))
    for q in range(NQ):
        cols = slice(q * WIDE, (q + 1) * WIDE)
        wait_bytes(home.at[q], recv_sem.at[S6 + q])
        for g in range(PAIRS // 8):
            sums = jnp.dot(
                to_rows.astype(BF16),
                home[q, g * 8 : (g + 1) * 8].reshape(LANES, WIDE),
                preferred_element_type=F32,
            ).reshape(OWNED, 16, WIDE)
            rows = slice(g * 16, (g + 1) * 16)
            out_ref[:, rows, cols] = (sums + 1.0 * c_ref[:, rows, cols]) * inverse[g]
        pltpu.make_async_copy(
            out_ref.at[:, :, cols], out_hbm.at[:, :, cols], out_sem.at[q]
        ).start()

    others = pl.ds(0, n - 1)
    wait_bytes(rq.at[others], send_sem.at[REQ])
    wait_bytes(gap_lo.at[pl.ds(0, low - 1)], send_sem.at[GAP_LO])
    wait_bytes(gap_hi.at[pl.ds(0, across - 1)], send_sem.at[GAP_HI])
    wait_bytes(w_back.at[others], send_sem.at[W4])
    wait_bytes(w_final.at[others], send_sem.at[W6])
    wait_bytes(held.at[0, others], send_sem.at[S1])
    wait_bytes(held.at[rest, others], send_sem.at[S1_REST])
    for q in range(NQ):
        wait_bytes(pick.at[q, others], send_sem.at[S3 + q])
        wait_bytes(back.at[q, others], send_sem.at[S4 + q])
        wait_bytes(final.at[q, others], send_sem.at[S6 + q])
    for q in range(NQ):
        cols = slice(q * WIDE, (q + 1) * WIDE)
        pltpu.make_async_copy(
            out_ref.at[:, :, cols], out_hbm.at[:, :, cols], out_sem.at[q]
        ).wait()


def hand_on(x_hbm, o_hbm, held, in_sem, out_sem):
    rows = [pl.ds(b * CBLK, CBLK) for b in range(OWNED)]
    into = [pltpu.make_async_copy(x_hbm.at[rows[b]], held.at[b], in_sem.at[b]) for b in range(OWNED)]
    out = [pltpu.make_async_copy(held.at[b], o_hbm.at[rows[b]], out_sem.at[b]) for b in range(OWNED)]
    for b in range(OWNED):
        into[b].start()
    for b in range(OWNED):
        into[b].wait()
        out[b].start()
    for b in range(OWNED):
        out[b].wait()


def on_device(n, nx, points, centroids, cand_peer, cand_block):
    rp = PAIRS // n
    pts, width = points.shape
    smem = pl.BlockSpec(memory_space=pltpu.SMEM)
    n_sem = 7 + 3 * NQ
    low = 16 if n >= 64 else 4
    hbm = pl.BlockSpec(memory_space=pl.ANY)
    refined = pl.pallas_call(
        functools.partial(kernel, n, nx, pts * n * nx),
        out_shape=jax.ShapeDtypeStruct((OWNED, CBLK, width), F32),
        in_specs=[hbm, hbm, smem, smem],
        out_specs=hbm,
        scratch_shapes=[
            pltpu.VMEM((1, LANES), F32),
            pltpu.VMEM((OWNED, CBLK, width), F32),
            pltpu.VMEM((pts, width), BF16),
            pltpu.VMEM((OWNED, CBLK, width), F32),
            pltpu.VMEM((n, 1, LANES), F32),
            pltpu.VMEM((n, SLOTS, n * ROWS), BF16),
            pltpu.VMEM((n * ROWS, n * SLOTS), BF16),
            pltpu.VMEM((NQ, PAIRS, ROWS, WIDE), BF16),
            pltpu.VMEM((NQ, n, rp, ROWS, WIDE), BF16),
            pltpu.VMEM((NQ, n, rp, SLOTS, WIDE), BF16),
            pltpu.VMEM((NQ, PAIRS, SLOTS, WIDE), BF16),
            pltpu.VMEM((NBLK, PAIRS, 8, LANES), F32),
            pltpu.VMEM((NBLK, PAIRS, 8, PBLK), F32),
            pltpu.VMEM((NBLK, PAIRS * 8, PBLK), BF16),
            pltpu.VMEM((NBLK * LANES, NBLK * LANES), BF16),
            pltpu.VMEM((NQ, PAIRS, SLOTS, WIDE), BF16),
            pltpu.VMEM((NQ, n, rp, SLOTS, WIDE), BF16),
            pltpu.VMEM((NQ, n, rp, ROWS, WIDE), BF16),
            pltpu.VMEM((NQ, PAIRS, ROWS, WIDE), BF16),
            pltpu.VMEM((PAIRS // 4, 1, LANES), F32),
            pltpu.VMEM((n, max(1, rp // 4), 1, LANES), F32),
            pltpu.VMEM((n, 1, LANES), F32),
            pltpu.VMEM((n, 1, LANES), F32),
            pltpu.VMEM((2, 1, LANES), F32),
            pltpu.VMEM((low, 1, LANES), F32),
            pltpu.VMEM((n // low * nx, 1, LANES), F32),
            pltpu.SemaphoreType.DMA((n_sem,)),
            pltpu.SemaphoreType.DMA((n_sem,)),
            pltpu.SemaphoreType.DMA((2,)),
            pltpu.SemaphoreType.DMA((NQ,)),
        ],
        compiler_params=pltpu.CompilerParams(
            collective_id=0, has_side_effects=True, vmem_limit_bytes=VMEM_LIMIT
        ),
    )(points, centroids.reshape(OWNED, CBLK, width), cand_peer, cand_block)
    return pl.pallas_call(
        hand_on,
        out_shape=jax.ShapeDtypeStruct((OWNED * CBLK, width), F32),
        in_specs=[hbm],
        out_specs=hbm,
        scratch_shapes=[
            pltpu.VMEM((OWNED, CBLK, width), F32),
            pltpu.SemaphoreType.DMA((OWNED,)),
            pltpu.SemaphoreType.DMA((OWNED,)),
        ],
    )(refined.reshape(OWNED * CBLK, width))


def solution(mesh):
    placed = P(("shard", "sub"), None)
    body = functools.partial(on_device, mesh.shape["shard"], mesh.shape["sub"])
    return jax.shard_map(
        body, mesh=mesh, in_specs=(placed,) * 4, out_specs=placed, check_vma=False
    )
```
